32 devices in a mesh: section: 4 (over z), space: 8 (over y, x, core).
Axes of the slice: x: 2, y: 2, z: 4, core: 2. Of those that a mesh axis runs over, the one named last changes fastest.
Arguments:
- inputs: bfloat16 [4, 64, 8, 2, 128], P(None, None, 'space'), may hold values from -6 to 6
- cotangent: bfloat16 [4, 64, 8, 2, 128], P(None, None, 'space'), may hold values from -6 to 6
- conv_weight: bfloat16 [2, 4, 128, 1728], P(None, 'section'), may hold values from -0.15625 to 0.15625
- mix_weight: bfloat16 [2, 4, 64, 128], P(None, 'section'), may hold values from -0.5 to 0.5
Outputs:
- conv_grad: float32 [2, 4, 128, 1728], P(None, 'section')
- mix_grad: float32 [2, 4, 64, 128], P(None, 'section')
The draws below stay inside these ranges and needn't reach their ends.
All inputs are finite; a program needn't handle non-finite values.
Results may differ from the reference program's by a relative error of at most 0.03.
Values may be sent and summed in bfloat16 or wider, within the bound.
No kernel may reach another device: no remote copies, remote signals or barrier semaphores. Data moves between devices by JAX's collectives and lax.ppermute only.
A program may use at most 64 MiB of HBM per device.

```python
import math
import jax
import jax.numpy as jnp
from jax import lax

CH = 64
HID = 128
NZ = 128
NY = 2
MB = 4
V = 2
SECTIONS = 4
NX = 8


def block_levels(rng, extent, cuts, least, high):
    def one(dim, shards_of):
        draws = jax.random.uniform(jax.random.fold_in(jax.random.fold_in(rng, 6), dim), (shards_of,), jnp.float32, least / len(cuts), high / len(cuts))
        return jnp.repeat(jnp.exp(draws), extent[dim] // shards_of).reshape((-1,) + (1,) * (len(extent) - dim - 1))

    factor_of = one(*cuts[0])
    for cut in cuts[1:]:
        factor_of = factor_of * one(*cut)
    return factor_of


def noise(rng, dims, scale, most, split=(), held_as=jnp.bfloat16):
    entries = jax.random.normal(rng, dims, jnp.float32) * scale
    if len(split) > 0:
        entries = block_levels(rng, dims, split, -0.22, 0.18) * entries
    return jnp.clip(entries, min=-most, max=most).astype(held_as)


def setup_inputs(seed: int = 0) -> dict:
    seeds = jax.random.split(jax.random.key(seed), 5)
    return {
        "inputs": noise(seeds[0], (MB, CH, NX, NY, NZ), 1.0, 6.0, ((2, 8),)),
        "cotangent": noise(seeds[1], (MB, CH, NX, NY, NZ), 1.0, 6.0, ((2, 8),)),
        "conv_weight": noise(seeds[2], (V, SECTIONS, HID, 27 * CH), (27 * CH) ** -0.5, 0.15625, ((1, 4),)),
        "mix_weight": noise(seeds[3], (V, SECTIONS, CH, HID), HID ** -0.5, 0.5, ((1, 4),)),
    }


def columns(padded, flip_sign, extent_x, extent_y, extent_z):
    pieces = []
    for step_x in (-1, 0, 1):
        for step_y in (-1, 0, 1):
            for step_z in (-1, 0, 1):
                start_x = 1 + flip_sign * step_x
                start_y = 1 + flip_sign * step_y
                start_z = 1 + flip_sign * step_z
                pieces.append(padded[:, start_x:start_x + extent_x, start_y:start_y + extent_y, start_z:start_z + extent_z])
    stacked = jnp.stack(pieces, 0)
    return stacked.reshape(27 * padded.shape[0], extent_x * extent_y * extent_z)

def silu_slope(preact):
    sigmoid_val = jax.nn.sigmoid(preact)
    return sigmoid_val * (1.0 + preact * (1.0 - sigmoid_val))

def transpose_conv(conv_w, channels):
    hidden_count = conv_w.shape[0]
    return conv_w.reshape(hidden_count, 27, channels).transpose(2, 1, 0).reshape(channels, 27 * hidden_count)

def padded_of(field):
    return jnp.pad(field, ((0, 0), (1, 1), (1, 1), (1, 1)))

def reference(inputs, cotangent, conv_weight, mix_weight):
    layer_groups = conv_weight.shape[0]
    section_count = conv_weight.shape[1]
    layer_count = layer_groups * section_count
    conv_all = conv_weight.reshape(layer_count, HID, 27 * CH)
    mix_all = mix_weight.reshape(layer_count, CH, HID)
    cell_count = NX * NY * NZ

    def forward_step(activation, weights):
        conv_w, mix_w = weights
        act_low = activation.astype(jnp.bfloat16)
        window = columns(padded_of(act_low), 1, NX, NY, NZ)
        preact = jnp.dot(conv_w, window, preferred_element_type=jnp.float32)
        hidden = jax.nn.silu(preact).astype(jnp.bfloat16)
        mixed_term = jnp.dot(mix_w, hidden, preferred_element_type=jnp.float32)
        result = activation.reshape(CH, cell_count) + mixed_term
        return (result.reshape(CH, NX, NY, NZ), act_low)

    def backward_step(upstream, layer_pack):
        conv_w, mix_w, act_low = layer_pack
        window = columns(padded_of(act_low), 1, NX, NY, NZ)
        preact = jnp.dot(conv_w, window, preferred_element_type=jnp.float32)
        hidden = jax.nn.silu(preact).astype(jnp.bfloat16)
        flat_up = upstream.reshape(CH, cell_count)
        up_low = flat_up.astype(jnp.bfloat16)
        mix_term = jnp.dot(up_low, hidden.T, preferred_element_type=jnp.float32)
        hid_grad = jnp.dot(mix_w.T, up_low, preferred_element_type=jnp.float32)
        pre_grad = (hid_grad * silu_slope(preact)).astype(jnp.bfloat16)
        conv_term = jnp.dot(pre_grad, window.T, preferred_element_type=jnp.float32)
        back_window = columns(padded_of(pre_grad.reshape(HID, NX, NY, NZ)), -1, NX, NY, NZ)
        spread = jnp.dot(transpose_conv(conv_w, CH), back_window, preferred_element_type=jnp.float32)
        downstream = flat_up + spread
        return (downstream.reshape(CH, NX, NY, NZ), (conv_term, mix_term))

    def one_micro(totals, micro_pair):
        source, seed_grad = micro_pair
        final_act, saved = lax.scan(forward_step, source.astype(jnp.float32), (conv_all, mix_all))
        first_up, layer_terms = lax.scan(backward_step, seed_grad.astype(jnp.float32), (conv_all, mix_all, saved), reverse=True)
        return ((totals[0] + layer_terms[0], totals[1] + layer_terms[1]), None)
    start_totals = (jnp.zeros((layer_count, HID, 27 * CH), jnp.float32), jnp.zeros((layer_count, CH, HID), jnp.float32))
    totals, unused = lax.scan(one_micro, start_totals, (inputs, cotangent))
    factor = 1.0 / math.sqrt(MB * NX * NY * NZ)
    conv_grad = (totals[0] * factor).reshape(layer_groups, section_count, HID, 27 * CH)
    mix_grad = (totals[1] * factor).reshape(layer_groups, section_count, CH, HID)
    return (conv_grad, mix_grad)
```

```python
import functools
import math

import jax
import jax.numpy as jnp
from jax import lax
from jax.experimental import pallas as pl
from jax.experimental.pallas import tpu as pltpu
from jax.sharding import PartitionSpec as P

BF = jnp.bfloat16
F32 = jnp.float32
NT = (((1,), (1,)), ((), ()))
NN = (((1,), (0,)), ((), ()))
TN = (((0,), (0,)), ((), ()))


def dot(a, b, dims):
    return lax.dot_general(a, b, dims, preferred_element_type=F32)


def swap_halves(x):
    return pltpu.roll(x, x.shape[1] // 2, 1)


def fold_piece(group, low, put):
    for dx in range(3):
        for dz in range(3):
            mid = 9 * dx + 3 + dz
            first, last = mid - 3, mid + 3
            at = 3 * dx + dz
            if mid % 2:
                row_one = jnp.where(low, group(first // 2), group(mid // 2))
                row_zero = swap_halves(jnp.where(low, group(last // 2), group(mid // 2)))
            else:
                row_zero = jnp.where(low, group(mid // 2), group(last // 2))
                row_one = swap_halves(jnp.where(low, group(mid // 2), group(first // 2)))
            put(at, row_zero, row_one)
    mixed = jnp.where(low, 0.0, group(13))
    put(9, swap_halves(mixed), mixed)


def unfold_terms(block, low):
    parts = {}
    for dx in range(3):
        for dz in range(3):
            mid = 9 * dx + 3 + dz
            zero, one = block(3 * dx + dz)
            if mid % 2:
                zero = swap_halves(zero)
            else:
                one = swap_halves(one)
            parts[mid] = zero + one
            parts[mid - 3] = one
            parts[mid + 3] = zero
    zero, one = block(9)
    parts[27] = swap_halves(zero) + one
    return [jnp.where(low, parts[2 * h], parts[2 * h + 1]) for h in range(14)]


def shifted(x, step, length):
    rows = x.shape[0]
    place = lax.broadcasted_iota(jnp.int32, x.shape, 0) % length
    edge = 0 if step > 0 else length - 1
    return jnp.where(place == edge, 0.0, pltpu.roll(x, step % rows, 0))


def fold_weights(me_ref, own_conv, own_mix, pieces, own_cat, folded, group_index):
    section, place, sections = me_ref[0], me_ref[1], folded.shape[0]
    hidden = own_cat.shape[0]
    shard = hidden // len(pieces)
    own_cat[:, : own_conv.shape[-1]] = own_conv[group_index, 0]
    own_cat[:, own_conv.shape[-1] :] = own_mix[group_index, 0].astype(F32).T.astype(BF)
    low = lax.broadcasted_iota(jnp.int32, (shard, 128), 1) < 64

    def one(layer, row, source):
        cache = {}

        def group(h):
            if h not in cache:
                cache[h] = source[:, 128 * h : 128 * h + 128].astype(F32)
            return cache[h]

        def put(at, zero, one_):
            folded[layer, pl.ds(row, shard), 128 * at : 128 * at + 128] = zero.astype(BF)
            folded[layer, pl.ds(hidden + row, shard), 128 * at : 128 * at + 128] = one_.astype(BF)

        fold_piece(group, low, put)

    def own_step(q, carry):
        row = pl.multiple_of(q * shard, shard)
        one(section, row, own_cat.at[pl.ds(row, shard)])
        return carry

    lax.fori_loop(0, len(pieces), own_step, 0)
    for rel, piece in enumerate(pieces):
        row = pl.multiple_of((place ^ rel) * shard, shard)

        def step(d, carry, piece=piece, row=row):
            layer = lax.rem(section + sections - 1 - d, sections)
            one(layer, row, piece.at[d])
            return carry

        lax.fori_loop(0, sections - 1, step, 0)


def columns_of(padded):
    planes = padded.shape[0] - 2
    parts = [padded[d : d + planes] for d in range(3)]
    return jnp.concatenate(parts, axis=2).reshape(planes * padded.shape[1], 3 * padded.shape[2])


def forward_layer(layer, section, act, padded, folded, slope, keep_a, keep_h):
    planes = padded.shape[0] - 2
    length = padded.shape[1]
    now = act[...]
    for at, value in enumerate((shifted(now, 1, length), now, shifted(now, -1, length))):
        padded[1 : planes + 1, :, 128 * at : 128 * at + 128] = value.astype(BF).reshape(planes, length, 128)
    pre = dot(columns_of(padded), folded[layer, :, :1152], NT)
    gate = jax.nn.sigmoid(pre)
    hidden = (pre * gate).astype(BF)
    slope[layer] = gate * (1.0 + pre * (1.0 - gate))
    act[...] = now + dot(hidden, folded[layer, :, 1152:], NN)

    @pl.when(layer == section)
    def _():
        keep_a[...] = padded[...]
        keep_h[...] = hidden


def backward_layer(layer, section, up, wide, folded, slope, keep_a, keep_h, terms, spread_if):
    planes = wide.shape[0] - 2
    length = wide.shape[1]
    now = up[...]
    up_low = now.astype(BF)
    grad = (dot(up_low, folded[layer, :, 1152:], NT) * slope[layer]).astype(BF)

    @pl.when(layer == section)
    def _():
        conv = dot(grad, columns_of(keep_a), TN)
        mix = dot(keep_h[...], up_low, TN)
        hidden = conv.shape[0] // 2
        low = lax.broadcasted_iota(jnp.int32, (hidden, 128), 1) < 64

        def block(at):
            full = mix if at == 9 else conv[:, 128 * at : 128 * at + 128]
            return full[:hidden], full[hidden:]

        for h, value in enumerate(unfold_terms(block, low)):
            terms[:, 128 * h : 128 * h + 128] = value

    def spread():
        wide[1 : planes + 1] = dot(grad, folded[layer, :, :1152], NN).reshape(planes, length, 1152)
        total = now
        for dz in range(3):
            part = 0.0
            for dx in range(3):
                at = 128 * (3 * dx + dz)
                part = part + wide[2 - dx : 2 - dx + planes, :, at : at + 128]
            part = part.reshape(planes * length, 128)
            total = total + (part if dz == 1 else shifted(part, dz - 1, length))
        up[...] = total

    if spread_if is None:
        spread()
    else:
        pl.when(spread_if)(spread)


def clear_edges(ref):
    ref[0] = jnp.zeros(ref.shape[1:], ref.dtype)
    ref[ref.shape[0] - 1] = jnp.zeros(ref.shape[1:], ref.dtype)


def place_planes(place, pieces, which, target):
    for rel, piece in enumerate(pieces):
        block = piece[which]
        rows = block.shape[0]
        target[pl.ds(pl.multiple_of((place ^ rel) * rows, rows), rows)] = block.astype(F32)


def first_kernel(shards, fields, me_ref, own_conv, own_mix, *refs):
    pieces, refs = refs[:shards], refs[shards:]
    planes, refs = refs[:fields], refs[fields:]
    act, folded, slope, keep_a, keep_h, own_cat, padded = refs
    fold_weights(me_ref, own_conv, own_mix, pieces, own_cat, folded, 0)
    place_planes(me_ref[1], planes, 0, act)
    clear_edges(padded)

    def step(layer, carry):
        forward_layer(layer, me_ref[0], act, padded, folded, slope, keep_a, keep_h)
        return carry

    lax.fori_loop(0, folded.shape[0], step, 0)


def store_terms(me_ref, terms, out):
    rows = out.shape[0]
    out[...] = terms[pl.ds(pl.multiple_of(me_ref[2] * rows, rows), rows)].astype(BF)


def middle_kernel(shards, fields, group_index, me_ref, own_conv, own_mix, act_in, *refs):
    pieces, refs = refs[:shards], refs[shards:]
    planes, refs = refs[:fields], refs[fields:]
    up, out, folded, slope, keep_a, keep_h, own_cat, padded, act, wide, terms = refs
    fold_weights(me_ref, own_conv, own_mix, pieces, own_cat, folded, group_index)
    act[...] = act_in[...]
    clear_edges(padded)
    clear_edges(wide)
    sections = folded.shape[0]

    def step(layer, carry):
        forward_layer(layer, me_ref[0], act, padded, folded, slope, keep_a, keep_h)
        return carry

    lax.fori_loop(0, sections, step, 0)
    place_planes(me_ref[1], planes, 1, up)

    def back(i, carry):
        backward_layer(sections - 1 - i, me_ref[0], up, wide, folded, slope, keep_a, keep_h, terms, None)
        return carry

    lax.fori_loop(0, sections, back, 0)
    store_terms(me_ref, terms, out)


def last_kernel(me_ref, up_in, folded, slope, keep_a, keep_h, out, up, wide, terms):
    up[...] = up_in[...]
    clear_edges(wide)
    sections = folded.shape[0]

    def back(i, carry):
        layer = sections - 1 - i
        backward_layer(layer, me_ref[0], up, wide, folded, slope, keep_a, keep_h, terms, layer > 0)
        return carry

    lax.fori_loop(0, sections, back, 0)
    store_terms(me_ref, terms, out)


def finish_kernel(groups, replicas, factor, me_ref, *refs):
    pieces, (conv, mix, whole) = refs[: groups * replicas], refs[groups * replicas :]
    wide = conv.shape[-1]
    for group in range(groups):
        for rel in range(replicas):
            piece = pieces[group * replicas + rel]
            rows = piece.shape[0]
            whole[pl.ds(pl.multiple_of((me_ref[2] ^ rel) * rows, rows), rows)] = piece[...].astype(F32) * factor
        conv[group, 0] = whole[:, :wide]
        mix[group, 0] = whole[:, wide:].T


def call(kernel, outs, scratch, smem, *args):
    vmem = pl.BlockSpec(memory_space=pltpu.VMEM)
    return pl.pallas_call(
        kernel,
        out_shape=outs,
        in_specs=[pl.BlockSpec(memory_space=pltpu.SMEM)] + [vmem] * len(args),
        out_specs=jax.tree.map(lambda _: vmem, outs),
        scratch_shapes=scratch,
        compiler_params=pltpu.CompilerParams(vmem_limit_bytes=60 * 1024 * 1024),
    )(smem, *args)


def exchange(block, axis, mask):
    count = lax.axis_size(axis)
    return lax.ppermute(block, axis, [(i, i ^ mask) for i in range(count)])


def per_device(inputs, cotangent, conv_weight, mix_weight):
    micro_count, channels, extent_x, extent_y, extent_z = inputs.shape
    layer_groups, _, hidden, taps = conv_weight.shape
    sections = lax.axis_size("section")
    space = lax.axis_size("space")
    section = lax.axis_index("section")
    place = lax.axis_index("space")
    replicas = space // micro_count
    shards = min(space, hidden // 16)
    shard = hidden // shards
    width = taps + channels
    cells = extent_x * space * extent_z
    lanes = extent_y * channels
    micro = place // replicas
    replica = place % replicas
    me = jnp.stack([section, place, replica]).astype(jnp.int32)

    start = (place % shards) * shard
    conv_rows = lax.dynamic_slice_in_dim(conv_weight[:, 0], start, shard, axis=1)
    mix_rows = lax.dynamic_slice_in_dim(jnp.swapaxes(mix_weight[:, 0], 1, 2), start, shard, axis=1)
    rows = jnp.concatenate([conv_rows, mix_rows], axis=2)
    gathered = []
    for group in range(layer_groups):
        mine = rows[group]
        route = [[(i, (i + d) % sections) for i in range(sections)] for d in range(1, sections)]
        passed = jnp.stack([lax.ppermute(mine, "section", r) for r in route])
        outer = [passed] + [exchange(passed, "space", 2 * k) for k in range(1, shards // 2)]
        pieces = []
        for piece in outer:
            pieces += [piece, exchange(piece, "space", 1)]
        gathered.append(pieces)

    both = jnp.stack([inputs, cotangent], axis=1)
    both = both.transpose(0, 1, 3, 5, 4, 2).reshape(micro_count, 2, extent_x * extent_z, lanes)
    near = []
    for k in range(micro_count):
        part = lax.dynamic_index_in_dim(both, micro ^ k, 0, keepdims=False)
        near.append(part if k == 0 else exchange(part, "space", k * replicas))
    near = jnp.stack(near)
    fields = [near] + [exchange(near, "space", r) for r in range(1, replicas)]
    planes = [fields[rel % replicas][rel // replicas] for rel in range(space)]

    def arr(*shape, dtype=F32):
        return jax.ShapeDtypeStruct(shape, dtype)

    def vm(shape):
        return pltpu.VMEM(shape.shape, shape.dtype)

    total_x = extent_x * space
    act = arr(cells, lanes)
    folded = arr(sections, 2 * hidden, 10 * lanes, dtype=BF)
    slope = arr(sections, cells, 2 * hidden)
    padded = arr(total_x + 2, extent_z, 3 * lanes, dtype=BF)
    keep_h = arr(cells, 2 * hidden, dtype=BF)
    own_cat = arr(hidden, width, dtype=BF)
    wide = arr(total_x + 2, extent_z, 9 * lanes)
    terms = arr(hidden, width)
    out = arr(hidden // replicas, width, dtype=BF)

    first = call(
        functools.partial(first_kernel, shards, space),
        [act, folded, slope, padded, keep_h],
        [vm(own_cat), vm(padded)],
        me, conv_weight, mix_weight, *gathered[0], *planes,
    )
    up, late = call(
        functools.partial(middle_kernel, shards, space, layer_groups - 1),
        [act, out],
        [vm(folded), vm(slope), vm(padded), vm(keep_h), vm(own_cat), vm(padded), vm(act), vm(wide), vm(terms)],
        me, conv_weight, mix_weight, first[0], *gathered[1], *planes,
    )
    early = call(last_kernel, out, [vm(act), vm(wide), vm(terms)], me, up, *first[1:])

    def reduce(part):
        level = [part] + [exchange(part, "space", k * replicas) for k in range(1, micro_count)]
        level = [x.astype(F32) for x in level]
        while len(level) > 1:
            level = [level[i] + level[i + 1] for i in range(0, len(level), 2)]
        mine = level[0].astype(BF)
        return [mine] + [exchange(mine, "space", r) for r in range(1, replicas)]

    pieces = []
    for part in (early, late):
        pieces += reduce(part)
    factor = 1.0 / math.sqrt(micro_count * cells * extent_y)
    return call(
        functools.partial(finish_kernel, layer_groups, replicas, factor),
        [arr(layer_groups, 1, hidden, taps), arr(layer_groups, 1, channels, hidden)],
        [vm(terms)],
        me, *pieces,
    )


def solution(mesh):
    placed = (
        P(None, None, "space", None, None),
        P(None, None, "space", None, None),
        P(None, "section", None, None),
        P(None, "section", None, None),
    )
    return jax.shard_map(
        per_device,
        mesh=mesh,
        in_specs=placed,
        out_specs=(P(None, "section", None, None), P(None, "section", None, None)),
        check_vma=False,
    )
```

```python
import functools
import math

import jax
import jax.numpy as jnp
from jax import lax
from jax.experimental import pallas as pl
from jax.experimental.pallas import tpu as pltpu
from jax.sharding import PartitionSpec as P

BF = jnp.bfloat16
F32 = jnp.float32
NT = (((1,), (1,)), ((), ()))
NN = (((1,), (0,)), ((), ()))
TN = (((0,), (0,)), ((), ()))
MIB = 1024 * 1024


def dot(a, b, dims):
    return lax.dot_general(a, b, dims, preferred_element_type=F32)


def shifted(x, step, length):
    place = lax.broadcasted_iota(jnp.int32, x.shape, 0) % length
    edge = 0 if step > 0 else length - 1
    return jnp.where(place == edge, 0.0, pltpu.roll(x, step % x.shape[0], 0))


def fold_taps(source, start, first, count, layer, folded):
    for tap in range(first, first + count):
        row = start + 64 * (tap - first)
        block = source[row : row + 64]
        if tap == 27:
            at, places = 1152, [(0, 0), (1, 1)]
            for y, other in ((0, 1), (1, 0)):
                folded[layer, at + 64 * y : at + 64 * y + 64, 128 * other : 128 * other + 128] = jnp.zeros_like(block)
        else:
            at = 128 * (3 * (tap // 9) + tap % 3)
            places = [[(0, 1)], [(0, 0), (1, 1)], [(1, 0)]][tap // 3 % 3]
        for y, other in places:
            folded[layer, at + 64 * y : at + 64 * y + 64, 128 * other : 128 * other + 128] = block


def columns_of(padded):
    planes = padded.shape[0] - 2
    parts = [padded[d : d + planes] for d in range(3)]
    return jnp.concatenate(parts, axis=2).reshape(planes * padded.shape[1], 3 * padded.shape[2])


def forward_layer(layer, slot, act, folded, slope, keep_a, keep_h):
    padded = keep_a.at[slot]
    planes = padded.shape[0] - 2
    length = padded.shape[1]
    now = act[...]
    for at, value in enumerate((shifted(now, 1, length), now, shifted(now, -1, length))):
        padded[1 : planes + 1, :, 128 * at : 128 * at + 128] = value.astype(BF).reshape(planes, length, 128)
    pre = dot(columns_of(padded), folded[layer, :1152], NN)
    gate = 0.5 * jnp.tanh(0.5 * pre) + 0.5
    wide = pre * gate
    hidden = wide.astype(BF)
    slope[layer] = (gate + wide * (1.0 - gate)).astype(slope.dtype)
    act[...] = now + dot(hidden, folded[layer, 1152:], NT)
    keep_h[slot] = hidden


def term_rows(conv, mix, terms):
    def block(at, y, other):
        return conv[at + 64 * y : at + 64 * y + 64, 128 * other : 128 * other + 128]

    for dx in range(3):
        for dz in range(3):
            row = 64 * (9 * dx + 3 + dz)
            at = 128 * (3 * dx + dz)
            terms[row : row + 64] = (block(at, 0, 0) + block(at, 1, 1)).astype(BF)
            terms[row - 192 : row - 128] = block(at, 0, 1).astype(BF)
            terms[row + 192 : row + 256] = block(at, 1, 0).astype(BF)
    terms[1728:1792] = (mix[:64, :128] + mix[64:, 128:]).astype(BF)


def backward_layer(layer, owned, up, wide, folded, slope, keep_a, keep_h, terms, spread_if):
    planes = wide.shape[0] - 2
    length = wide.shape[1]
    now = up[...]
    up_low = now.astype(BF)
    grad = (dot(up_low, folded[layer, 1152:], NN) * slope[layer]).astype(BF)

    @pl.when(owned)
    def _():
        conv = dot(columns_of(keep_a.at[0]), grad, TN)
        term_rows(conv, dot(up_low, keep_h[0], TN), terms)

    @pl.when(spread_if)
    def _():
        wide[1 : planes + 1] = dot(grad, folded[layer, :1152], NT).reshape(planes, length, 1152)
        total = now
        for dz in range(3):
            part = 0.0
            for dx in range(3):
                at = 128 * (3 * dx + dz)
                part = part + wide[2 - dx : 2 - dx + planes, :, at : at + 128]
            part = part.reshape(planes * length, 128)
            total = total + (part if dz == 1 else shifted(part, dz - 1, length))
        up[...] = total


def clear_edges(ref):
    ref[0] = jnp.zeros(ref.shape[1:], ref.dtype)
    ref[ref.shape[0] - 1] = jnp.zeros(ref.shape[1:], ref.dtype)


def needed(plan, group, field):
    weight_steps, plane_steps = plan(0, 0, field)
    return sorted({step[0] for step in weight_steps[group] + plane_steps})


def take(plan, me_ref, field, group, conv, mix, pieces, folded, target):
    section, place = me_ref[0], me_ref[1]
    taps = conv.shape[2] // 64
    fold_taps(conv.at[group, 0], 0, 0, taps, section, folded)
    fold_taps(mix.at[group, 0], 0, taps, 1, section, folded)
    weight_steps, plane_steps = plan(section, place, field)
    pieces = dict(zip(needed(plan, group, field), pieces, strict=True))
    for piece, start, count, layer, first, choices in weight_steps[group]:
        for choice in choices:

            @pl.when(first == choice)
            def _(piece=piece, start=start, count=count, layer=layer, choice=choice):
                fold_taps(pieces[piece], start, choice, count, layer, folded)

    for piece, start, rows, rel in plane_steps:
        row = pl.multiple_of((place ^ rel) * rows, rows)
        target[pl.ds(row, rows)] = pieces[piece][start : start + rows].astype(F32)


def begin(copies, sems, first):
    started = []
    for number, (source, target) in enumerate(copies):
        copy = pltpu.make_async_copy(source, target, sems.at[first + number])
        copy.start()
        started.append(copy)
    return started


def finish(started):
    for copy in started:
        copy.wait()


def split_kernel(me_ref, inputs, cotangent, own, beside, across, swap):
    chip, core = me_ref[1] // 2, me_ref[1] % 2
    for number, source in enumerate((inputs, cotangent)):
        rows = slice(128 * number, 128 * number + 128)

        def turned(offset, source=source):
            return source[chip ^ offset].astype(F32).T.astype(BF)

        mine, far = turned(0), turned(3)
        one, two = turned(1 + core), turned(2 - core)
        own[rows] = mine
        across[rows] = far
        beside[rows] = one
        swap[rows] = mine
        swap[256 + 128 * number : 384 + 128 * number] = two


def first_kernel(plan, piece_count, me_ref, conv, mix, *refs):
    pieces, refs = refs[:piece_count], refs[piece_count:]
    act, folded, slope, keep_a, keep_h = refs
    section = me_ref[0]
    take(plan, me_ref, 0, 0, conv, mix, pieces, folded, act)
    for slot in range(2):
        clear_edges(keep_a.at[slot])

    def step(layer, carry):
        forward_layer(layer, jnp.where(layer == section, 0, 1), act, folded, slope, keep_a, keep_h)
        return carry

    lax.fori_loop(0, folded.shape[0], step, 0)


def all_back(section, last, up, wide, folded, slope, keep_a, keep_h, terms, replica, out):
    sections = folded.shape[0]

    def back(i, carry):
        layer = sections - 1 - i
        backward_layer(
            layer, layer == section, up, wide, folded, slope, keep_a, keep_h, terms, (layer >= 0) if last else layer > 0
        )
        return carry

    lax.fori_loop(0, sections, back, 0)
    rows = out.shape[0]
    out[...] = terms[pl.ds(pl.multiple_of(replica * rows, rows), rows)]


def second_kernel(plan, piece_count, me_ref, conv, mix, *refs):
    pieces, refs = refs[:piece_count], refs[piece_count:]
    act_in, up, out, folded, slope, keep_a, keep_h, act, wide, terms = refs
    section = me_ref[0]
    act[...] = act_in[...]
    take(plan, me_ref, 1, 1, conv, mix, pieces, folded, up)
    for slot in range(2):
        clear_edges(keep_a.at[slot])
    clear_edges(wide)

    def step(layer, carry):
        forward_layer(layer, jnp.where(layer == section, 0, 1), act, folded, slope, keep_a, keep_h)
        return carry

    lax.fori_loop(0, folded.shape[0], step, 0)
    all_back(section, True, up, wide, folded, slope, keep_a, keep_h, terms, me_ref[2], out)


def third_kernel(me_ref, up_in, folded, slope, keep_a, keep_h, out, up, wide, terms):
    up[...] = up_in[...]
    clear_edges(wide)
    all_back(me_ref[0], False, up, wide, folded, slope, keep_a, keep_h, terms, me_ref[2], out)


def send_grads(whole, conv, mix, group, start, stop, sems):
    taps = conv.shape[2]
    count = min(stop, taps) - start
    copies = [(whole.at[pl.ds(start, count)], conv.at[group, 0, pl.ds(start, count)])]
    if stop > taps:
        copies.append((whole.at[pl.ds(taps, stop - taps)], mix.at[group, 0]))
    return begin(copies, sems, 1 if start else 0)


def pair_kernel(group, factor, me_ref, own_a, own_b, far_a, far_b, *refs):
    conv, mix, whole, sems = refs[-4:]
    first = me_ref[2] == 0
    rows = own_a.shape[0]
    own = own_a[...].astype(F32) + own_b[...].astype(F32)
    far = far_a[...].astype(F32) + far_b[...].astype(F32)
    whole[:rows] = jnp.where(first, own, far) * factor
    started = send_grads(whole, conv, mix, group, 0, rows, sems)
    whole[rows:] = jnp.where(first, far, own) * factor
    started += send_grads(whole, conv, mix, group, rows, 2 * rows, sems)
    finish(started)


def plain_kernel(group, factor, me_ref, terms, *refs):
    conv, mix, whole, sems = refs[-4:]
    whole[...] = terms[...].astype(F32) * factor
    finish(send_grads(whole, conv, mix, group, 0, whole.shape[0], sems))


def size_of(x):
    return math.prod(x.shape) * x.dtype.itemsize


def call(kernel, outs, scratch, traffic, *args, into=()):
    vmem = pl.BlockSpec(memory_space=pltpu.VMEM)
    far = pl.BlockSpec(memory_space=pl.ANY)
    specs = [pl.BlockSpec(memory_space=pltpu.SMEM)] + [vmem] * (len(args) - 1) + [far] * len(into)
    held = sum(size_of(x) for x in scratch if x.memory_space == pltpu.VMEM)
    passed = sum(size_of(x) for x in args) + sum(size_of(x) for x in outs)
    limit = held + held // 4 + 10 * MIB
    if held + passed > 30 * MIB:
        limit = 63 * MIB
    return pl.pallas_call(
        kernel,
        out_shape=outs,
        in_specs=specs,
        out_specs=[far if kernel.func in (pair_kernel, plain_kernel) else vmem] * len(outs),
        scratch_shapes=scratch,
        input_output_aliases={len(args) + i: i for i in range(len(into))},
        compiler_params=pltpu.CompilerParams(vmem_limit_bytes=limit),
        cost_estimate=pl.CostEstimate(flops=traffic * 100, bytes_accessed=traffic, transcendentals=0),
    )(*args, *into)


def exchange(block, mask):
    count = lax.axis_size("space")
    return lax.ppermute(block, "space", [(i, i ^ mask) for i in range(count)])


def cross(block, first, second):
    count = lax.axis_size("space")
    return lax.ppermute(block, "space", [(i, i ^ (second if i % 2 else first)) for i in range(count)])


def after(x, *others):
    return lax.optimization_barrier((x, *others))[0]


def gather_paired(weights, fields, me, place):
    sections, space = lax.axis_size("section"), lax.axis_size("space")
    rows = weights.shape[1]
    half, quarter = rows // 2, rows // 4
    chip, core = place // 2, place % 2
    side = (chip // 2) ^ (chip % 2)
    mine = jnp.where(side == 0, weights[:, :half], weights[:, half:])
    part = lax.dynamic_slice_in_dim(mine, core * quarter, quarter, axis=1)
    route = []
    for s in range(sections):
        for j in range(space):
            target = (s + (-1 if j % 2 else 1)) % sections
            route.append((s * space + j, target * space + j))
    across = [(s, (s + 2) % sections) for s in range(sections)]
    own, beside, diagonal, swap = call(
        functools.partial(split_kernel),
        [jax.ShapeDtypeStruct((count, 128), BF) for count in (256, 256, 256, 512)],
        [], MIB, me, *fields,
    )
    other = exchange(swap, 1)
    diagonal = exchange(diagonal, 6)
    near = lax.ppermute(mine, ("section", "space"), route)
    far = lax.ppermute(part, "section", across)
    sent = [beside, other[256:]]
    pieces = []
    for group in range(2):
        here = jnp.concatenate([near[group], far[group]] + (sent if group == 0 else []), axis=0)
        there = cross(here, 2, 4)
        pieces += [here, there, exchange(here, 1), None if group else exchange(after(there, diagonal), 1)]
    planes = [own, other, diagonal, exchange(diagonal, 1)]
    plane_rows = 128

    def plan(section, place, field):
        chip, core = place // 2, place % 2
        side = (chip // 2) ^ (chip % 2)
        weight_steps = []
        for group in range(2):
            steps = []
            for swapped in range(2):
                source = core ^ swapped
                beside = lax.rem(section + sections - 1 + 2 * source, sections)
                across = lax.rem(section + 2, sections)
                for other in range(2):
                    piece = 4 * group + 2 * swapped + other
                    first = (side ^ other) * 14
                    steps.append((piece, 0, 14, beside, first, (0, 14)))
                    steps.append((piece, half, 7, across, first + source * 7, (0, 7, 14, 21)))
            weight_steps.append(steps)
        plane_steps = []
        start = field * plane_rows
        for piece, rel in ((8, 0), (9, 1), (10, 6), (11, 7)):
            plane_steps.append((piece, start, plane_rows, rel))
        for swapped in range(2):
            rel = swapped ^ (2 + 2 * (core ^ swapped))
            start = half + quarter + field * plane_rows
            plane_steps.append((1 + 2 * swapped, start, plane_rows, rel))
            plane_steps.append((1 + 2 * swapped, start + 2 * plane_rows, plane_rows, rel ^ 1))
        return weight_steps, plane_steps

    return pieces + planes, plan


def gather_plain(weights, both, place, replicas):
    sections = lax.axis_size("section")
    micro_count, _, plane_rows, _ = both.shape
    routes = [[(i, (i + d) % sections) for i in range(sections)] for d in range(1, sections)]
    pieces = [lax.ppermute(group, "section", route) for group in weights for route in routes]
    near = []
    for k in range(micro_count):
        part = lax.dynamic_index_in_dim(both, (place // replicas) ^ k, 0, keepdims=False)
        near.append(part if k == 0 else exchange(part, k * replicas))
    near = jnp.stack(near)
    fields = [near] + [exchange(near, r) for r in range(1, replicas)]
    fields = [x.reshape(-1, x.shape[-1]) for x in fields]

    def plan(section, place, field):
        first = weights.shape[0] * (sections - 1)
        weight_steps = [
            [
                (group * (sections - 1) + d - 1, 0, weights.shape[1] // 64, lax.rem(section + sections - d, sections), 0, (0,))
                for d in range(1, sections)
            ]
            for group in range(weights.shape[0])
        ]
        plane_steps = [
            (first + r, (2 * k + field) * plane_rows, plane_rows, k * replicas + r)
            for k in range(micro_count)
            for r in range(replicas)
        ]
        return weight_steps, plane_steps

    return pieces + fields, plan


def per_device(inputs, cotangent, conv_weight, mix_weight):
    micro_count, channels, extent_x, extent_y, extent_z = inputs.shape
    groups, _, hidden, taps = conv_weight.shape
    sections = lax.axis_size("section")
    space = lax.axis_size("space")
    section = lax.axis_index("section")
    place = lax.axis_index("space")
    replicas = space // micro_count
    width = taps + channels
    layers = groups * sections
    cells = extent_x * space * extent_z
    lanes = extent_y * channels
    paired = space == 8 and replicas == 2 and sections == 4 and extent_x == 1 and extent_z == 128 and lanes == 128
    me = jnp.stack([section, place, place % replicas]).astype(jnp.int32)

    conv_rows = jnp.swapaxes(conv_weight, 2, 3)
    weights = jnp.concatenate([conv_rows[:, 0], mix_weight[:, 0]], axis=1)
    if paired:
        fields = [x[:, :, 0].transpose(0, 2, 1, 3).reshape(micro_count, lanes, extent_z) for x in (inputs, cotangent)]
        pieces, plan = gather_paired(weights, fields, me, place)
    else:
        both = jnp.stack([inputs, cotangent], axis=1)
        both = both.transpose(0, 1, 3, 5, 4, 2).reshape(micro_count, 2, extent_x * extent_z, lanes)
        pieces, plan = gather_plain(weights, both, place, replicas)

    total_x = extent_x * space
    act = jax.ShapeDtypeStruct((cells, lanes), F32)
    kept = [
        jax.ShapeDtypeStruct((sections, 10 * lanes, 2 * hidden), BF),
        jax.ShapeDtypeStruct((sections, cells, 2 * hidden), BF),
        jax.ShapeDtypeStruct((2, total_x + 2, extent_z, 3 * lanes), BF),
        jax.ShapeDtypeStruct((2, cells, 2 * hidden), BF),
    ]
    early = [pieces[i] for i in needed(plan, 0, 0)]
    act, *saved = call(
        functools.partial(first_kernel, plan, len(early)),
        [act] + kept,
        [], 30 * MIB,
        me, conv_rows, mix_weight, *early,
    )
    if paired:
        pieces[7] = exchange(after(pieces[5], act), 1)
    late = [pieces[i] for i in needed(plan, 1, 1)]
    terms = jax.ShapeDtypeStruct((width // replicas, hidden), BF)
    wide = pltpu.VMEM((total_x + 2, extent_z, 9 * lanes), F32)
    whole = pltpu.VMEM((width, hidden), BF)
    up, late_terms = call(
        functools.partial(second_kernel, plan, len(late)),
        [act, terms],
        [pltpu.VMEM(x.shape, x.dtype) for x in kept] + [pltpu.VMEM((cells, lanes), F32), wide, whole],
        40 * MIB,
        me, conv_rows, mix_weight, *late, act,
    )
    traded = cross(late_terms, 2, 4) if paired else None
    (early_terms,) = call(
        functools.partial(third_kernel),
        [terms],
        [pltpu.VMEM((cells, lanes), F32), wide, whole],
        20 * MIB,
        me, up, *saved,
    )

    factor = 1.0 / math.sqrt(micro_count * cells * extent_y)
    outs = [
        jax.ShapeDtypeStruct((groups, 1, taps, hidden), F32),
        jax.ShapeDtypeStruct((groups, 1, channels, hidden), F32),
    ]
    scratch = [pltpu.VMEM((width, hidden), F32), pltpu.SemaphoreType.DMA((3,))]
    grads = ()
    for group in (1, 0):
        own = late_terms if group else early_terms
        if paired:
            met = after(traded, early_terms) if group else cross(own, 2, 4)
            half = (own.astype(F32) + met.astype(F32)).astype(BF)
            other = cross(half, 4, 2)
            if grads:
                other = after(other, grads[0])
            kernel, parts = pair_kernel, (half, other, exchange(half, 1), exchange(other, 1))
        else:
            level = [own] + [exchange(own, k * replicas) for k in range(1, micro_count)]
            level = [x.astype(F32) for x in level]
            while len(level) > 1:
                level = [level[i] + level[i + 1] for i in range(0, len(level), 2)]
            rows_of = [[m * replicas + r for r in range(replicas)] for m in range(micro_count)]
            every = lax.all_gather(level[0].astype(BF), "space", axis=0, tiled=True, axis_index_groups=rows_of)
            kernel, parts = plain_kernel, (every,)
        grads = call(functools.partial(kernel, group, factor), outs, scratch, 4 * MIB, me, *parts, into=grads)
    conv, mix = grads
    return (jnp.swapaxes(conv, 2, 3), mix)


def solution(mesh):
    placed = (
        P(None, None, "space", None, None),
        P(None, None, "space", None, None),
        P(None, "section", None, None),
        P(None, "section", None, None),
    )
    return jax.shard_map(
        per_device,
        mesh=mesh,
        in_specs=placed,
        out_specs=(P(None, "section", None, None), P(None, "section", None, None)),
        check_vma=False,
    )
```

```python
import functools
import math

import jax
import jax.numpy as jnp
from jax import lax
from jax.experimental import pallas as pl
from jax.experimental.pallas import tpu as pltpu
from jax.sharding import PartitionSpec as P

BF = jnp.bfloat16
F32 = jnp.float32
NT = (((1,), (1,)), ((), ()))
NN = (((1,), (0,)), ((), ()))
TN = (((0,), (0,)), ((), ()))
MIB = 1024 * 1024


def dot(a, b, dims):
    return lax.dot_general(a, b, dims, preferred_element_type=F32)


def shifted(x, step, length):
    place = lax.broadcasted_iota(jnp.int32, x.shape, 0) % length
    edge = 0 if step > 0 else length - 1
    return jnp.where(place == edge, 0.0, pltpu.roll(x, step % x.shape[0], 0))


def fold_taps(source, start, first, count, layer, folded):
    for tap in range(first, first + count):
        row = start + 64 * (tap - first)
        block = source[row : row + 64]
        if tap == 27:
            at, places = 1152, [(0, 0), (1, 1)]
            for y, other in ((0, 1), (1, 0)):
                folded[layer, at + 64 * y : at + 64 * y + 64, 128 * other : 128 * other + 128] = jnp.zeros_like(block)
        else:
            at = 128 * (3 * (tap // 9) + tap % 3)
            places = [[(0, 1)], [(0, 0), (1, 1)], [(1, 0)]][tap // 3 % 3]
        for y, other in places:
            folded[layer, at + 64 * y : at + 64 * y + 64, 128 * other : 128 * other + 128] = block


def columns_of(padded):
    planes = padded.shape[0] - 2
    parts = [padded[d : d + planes] for d in range(3)]
    return jnp.concatenate(parts, axis=2).reshape(planes * padded.shape[1], 3 * padded.shape[2])


def forward_layer(layer, slot, act, folded, slope, keep_a, keep_h):
    padded = keep_a.at[slot]
    planes = padded.shape[0] - 2
    length = padded.shape[1]
    now = act[...]
    for at, value in enumerate((shifted(now, 1, length), now, shifted(now, -1, length))):
        padded[1 : planes + 1, :, 128 * at : 128 * at + 128] = value.astype(BF).reshape(planes, length, 128)
    pre = dot(columns_of(padded), folded[layer, :1152], NN)
    gate = 0.5 * jnp.tanh(0.5 * pre) + 0.5
    wide = pre * gate
    hidden = wide.astype(BF)
    slope[layer] = (gate + wide * (1.0 - gate)).astype(slope.dtype)
    act[...] = now + dot(hidden, folded[layer, 1152:], NT)
    keep_h[slot] = hidden


def term_rows(conv, mix, terms):
    def block(at, y, other):
        return conv[at + 64 * y : at + 64 * y + 64, 128 * other : 128 * other + 128]

    for dx in range(3):
        for dz in range(3):
            row = 64 * (9 * dx + 3 + dz)
            at = 128 * (3 * dx + dz)
            terms[row : row + 64] = (block(at, 0, 0) + block(at, 1, 1)).astype(BF)
            terms[row - 192 : row - 128] = block(at, 0, 1).astype(BF)
            terms[row + 192 : row + 256] = block(at, 1, 0).astype(BF)
    terms[1728:1792] = (mix[:64, :128] + mix[64:, 128:]).astype(BF)


def backward_layer(layer, owned, up, wide, folded, slope, keep_a, keep_h, terms, spread_if):
    planes = wide.shape[0] - 2
    length = wide.shape[1]
    now = up[...]
    up_low = now.astype(BF)
    grad = (dot(up_low, folded[layer, 1152:], NN) * slope[layer]).astype(BF)

    @pl.when(owned)
    def _():
        conv = dot(columns_of(keep_a.at[0]), grad, TN)
        term_rows(conv, dot(up_low, keep_h[0], TN), terms)

    @pl.when(spread_if)
    def _():
        wide[1 : planes + 1] = dot(grad, folded[layer, :1152], NT).reshape(planes, length, 1152)
        total = now
        for dz in range(3):
            part = 0.0
            for dx in range(3):
                at = 128 * (3 * dx + dz)
                part = part + wide[2 - dx : 2 - dx + planes, :, at : at + 128]
            part = part.reshape(planes * length, 128)
            total = total + (part if dz == 1 else shifted(part, dz - 1, length))
        up[...] = total


def clear_edges(ref):
    ref[0] = jnp.zeros(ref.shape[1:], ref.dtype)
    ref[ref.shape[0] - 1] = jnp.zeros(ref.shape[1:], ref.dtype)


def needed(plan, group, field):
    weight_steps, plane_steps = plan(0, 0, field)
    return sorted({step[0] for step in weight_steps[group] + plane_steps})


def take(plan, me_ref, field, group, conv, mix, pieces, folded, target):
    section, place = me_ref[0], me_ref[1]
    taps = conv.shape[2] // 64
    fold_taps(conv.at[group, 0], 0, 0, taps, section, folded)
    fold_taps(mix.at[group, 0], 0, taps, 1, section, folded)
    weight_steps, plane_steps = plan(section, place, field)
    pieces = dict(zip(needed(plan, group, field), pieces, strict=True))
    for piece, start, count, layer, first, choices in weight_steps[group]:
        for choice in choices:

            @pl.when(first == choice)
            def _(piece=piece, start=start, count=count, layer=layer, choice=choice):
                fold_taps(pieces[piece], start, choice, count, layer, folded)

    for piece, start, rows, rel in plane_steps:
        row = pl.multiple_of((place ^ rel) * rows, rows)
        target[pl.ds(row, rows)] = pieces[piece][start : start + rows].astype(F32)


def begin(copies, sems, first):
    started = []
    for number, (source, target) in enumerate(copies):
        copy = pltpu.make_async_copy(source, target, sems.at[first + number])
        copy.start()
        started.append(copy)
    return started


def finish(started):
    for copy in started:
        copy.wait()


def split_kernel(me_ref, inputs, cotangent, token, own, beside, across, swap):
    chip, core = me_ref[1] // 2, me_ref[1] % 2
    old = lax.broadcasted_iota(jnp.int32, (128, 128), 0)
    new = lax.broadcasted_iota(jnp.int32, (128, 128), 1)
    order = ((old % 2) * 64 + old // 2 == new).astype(F32).astype(BF)
    for number, source in enumerate((inputs, cotangent)):
        rows = slice(128 * number, 128 * number + 128)

        def turned(offset, source=source):
            return dot(source[chip ^ offset], order, TN).astype(BF)

        mine, far = turned(0), turned(3)
        one, two = turned(1 + core), turned(2 - core)
        own[rows] = mine
        across[rows] = far
        beside[rows] = one
        swap[rows] = mine
        swap[256 + 128 * number : 384 + 128 * number] = two


def first_kernel(plan, piece_count, me_ref, conv, mix, *refs):
    pieces, refs = refs[:piece_count], refs[piece_count:]
    act, folded, slope, keep_a, keep_h = refs
    section = me_ref[0]
    take(plan, me_ref, 0, 0, conv, mix, pieces, folded, act)
    for slot in range(2):
        clear_edges(keep_a.at[slot])

    def step(layer, carry):
        forward_layer(layer, jnp.where(layer == section, 0, 1), act, folded, slope, keep_a, keep_h)
        return carry

    lax.fori_loop(0, folded.shape[0], step, 0)


def all_back(section, last, up, wide, folded, slope, keep_a, keep_h, terms, replica, out):
    sections = folded.shape[0]

    def back(i, carry):
        layer = sections - 1 - i
        backward_layer(
            layer, layer == section, up, wide, folded, slope, keep_a, keep_h, terms, (layer >= 0) if last else layer > 0
        )
        return carry

    lax.fori_loop(0, sections, back, 0)
    rows = out.shape[0]
    out[...] = terms[pl.ds(pl.multiple_of(replica * rows, rows), rows)]


def second_kernel(plan, piece_count, me_ref, conv, mix, *refs):
    pieces, refs = refs[:piece_count], refs[piece_count:]
    act_in, up, out, folded, slope, keep_a, keep_h, act, wide, terms = refs
    section = me_ref[0]
    act[...] = act_in[...]
    take(plan, me_ref, 1, 1, conv, mix, pieces, folded, up)
    for slot in range(2):
        clear_edges(keep_a.at[slot])
    clear_edges(wide)

    def step(layer, carry):
        forward_layer(layer, jnp.where(layer == section, 0, 1), act, folded, slope, keep_a, keep_h)
        return carry

    lax.fori_loop(0, folded.shape[0], step, 0)
    all_back(section, True, up, wide, folded, slope, keep_a, keep_h, terms, me_ref[2], out)


def third_kernel(me_ref, up_in, folded, slope, keep_a, keep_h, out, up, wide, terms):
    up[...] = up_in[...]
    clear_edges(wide)
    all_back(me_ref[0], False, up, wide, folded, slope, keep_a, keep_h, terms, me_ref[2], out)


def send_grads(whole, conv, mix, group, start, stop, sems):
    taps = conv.shape[2]
    count = min(stop, taps) - start
    copies = [(whole.at[pl.ds(start, count)], conv.at[group, 0, pl.ds(start, count)])]
    if stop > taps:
        copies.append((whole.at[pl.ds(taps, stop - taps)], mix.at[group, 0]))
    return begin(copies, sems, 1 if start else 0)


def pair_kernel(group, factor, me_ref, own_a, own_b, far_a, far_b, *refs):
    conv, mix, whole, sems = refs[-4:]
    first = me_ref[2] == 0
    rows = own_a.shape[0]
    own = own_a[...].astype(F32) + own_b[...].astype(F32)
    far = far_a[...].astype(F32) + far_b[...].astype(F32)
    whole[:rows] = jnp.where(first, own, far) * factor
    started = send_grads(whole, conv, mix, group, 0, rows, sems)
    whole[rows:] = jnp.where(first, far, own) * factor
    started += send_grads(whole, conv, mix, group, rows, 2 * rows, sems)
    finish(started)


def plain_kernel(group, factor, me_ref, terms, *refs):
    conv, mix, whole, sems = refs[-4:]
    whole[...] = terms[...].astype(F32) * factor
    finish(send_grads(whole, conv, mix, group, 0, whole.shape[0], sems))


def size_of(x):
    return math.prod(x.shape) * x.dtype.itemsize


def call(kernel, outs, scratch, traffic, *args, into=()):
    vmem = pl.BlockSpec(memory_space=pltpu.VMEM)
    far = pl.BlockSpec(memory_space=pl.ANY)
    specs = [pl.BlockSpec(memory_space=pltpu.SMEM)] + [vmem] * (len(args) - 1) + [far] * len(into)
    held = sum(size_of(x) for x in scratch if x.memory_space == pltpu.VMEM)
    passed = sum(size_of(x) for x in args) + sum(size_of(x) for x in outs)
    limit = held + held // 4 + 10 * MIB
    if held + passed > 30 * MIB:
        limit = 63 * MIB
    return pl.pallas_call(
        kernel,
        out_shape=outs,
        in_specs=specs,
        out_specs=[far if kernel.func in (pair_kernel, plain_kernel) else vmem] * len(outs),
        scratch_shapes=scratch,
        input_output_aliases={len(args) + i: i for i in range(len(into))},
        compiler_params=pltpu.CompilerParams(vmem_limit_bytes=limit),
        cost_estimate=pl.CostEstimate(flops=traffic * 100, bytes_accessed=traffic, transcendentals=0),
    )(*args, *into)


def exchange(block, mask):
    count = lax.axis_size("space")
    return lax.ppermute(block, "space", [(i, i ^ mask) for i in range(count)])


def cross(block, first, second):
    count = lax.axis_size("space")
    return lax.ppermute(block, "space", [(i, i ^ (second if i % 2 else first)) for i in range(count)])


def after(x, *others):
    return lax.optimization_barrier((x, *others))[0]


def gather_paired(weights, fields, me, place):
    sections, space = lax.axis_size("section"), lax.axis_size("space")
    rows = weights.shape[1]
    half, quarter = rows // 2, rows // 4
    chip, core = place // 2, place % 2
    side = (chip // 2) ^ (chip % 2)
    mine = jnp.where(side == 0, weights[:, :half], weights[:, half:])
    part = lax.dynamic_slice_in_dim(mine, core * quarter, quarter, axis=1)
    route = []
    for s in range(sections):
        for j in range(space):
            target = (s + (-1 if j % 2 else 1)) % sections
            route.append((s * space + j, target * space + j))
    across = [(s, (s + 2) % sections) for s in range(sections)]
    token = exchange(mine[0, :16], 1)
    own, beside, diagonal, swap = call(
        functools.partial(split_kernel),
        [jax.ShapeDtypeStruct((count, 128), BF) for count in (256, 256, 256, 512)],
        [], MIB, me, *fields, token,
    )
    other = exchange(swap, 1)
    diagonal = exchange(diagonal, 6)
    near, far = [], []
    for group in range(2):
        near.append(lax.ppermute(after(mine[group], *near), ("section", "space"), route))
        far.append(lax.ppermute(after(part[group], *near[:group]), "section", across))
    sent = [beside, other[256:]]
    diagonal_far = exchange(diagonal, 1)
    pieces = []
    for group in range(2):
        here = jnp.concatenate([near[group], far[group]] + (sent if group == 0 else []), axis=0)
        there = cross(here, 2, 4)
        pieces += [here, there, exchange(here, 1), None if group else exchange(after(there, diagonal, near[1], far[1]), 1)]
    planes = [own, other, diagonal, diagonal_far]
    plane_rows = 128

    def plan(section, place, field):
        chip, core = place // 2, place % 2
        side = (chip // 2) ^ (chip % 2)
        weight_steps = []
        for group in range(2):
            steps = []
            for swapped in range(2):
                source = core ^ swapped
                beside = lax.rem(section + sections - 1 + 2 * source, sections)
                across = lax.rem(section + 2, sections)
                for other in range(2):
                    piece = 4 * group + 2 * swapped + other
                    first = (side ^ other) * 14
                    steps.append((piece, 0, 14, beside, first, (0, 14)))
                    steps.append((piece, half, 7, across, first + source * 7, (0, 7, 14, 21)))
            weight_steps.append(steps)
        plane_steps = []
        start = field * plane_rows
        for piece, rel in ((8, 0), (9, 1), (10, 6), (11, 7)):
            plane_steps.append((piece, start, plane_rows, rel))
        for swapped in range(2):
            rel = swapped ^ (2 + 2 * (core ^ swapped))
            start = half + quarter + field * plane_rows
            plane_steps.append((1 + 2 * swapped, start, plane_rows, rel))
            plane_steps.append((1 + 2 * swapped, start + 2 * plane_rows, plane_rows, rel ^ 1))
        return weight_steps, plane_steps

    return pieces + planes, plan


def gather_plain(weights, both, place, replicas):
    sections = lax.axis_size("section")
    micro_count, _, plane_rows, _ = both.shape
    routes = [[(i, (i + d) % sections) for i in range(sections)] for d in range(1, sections)]
    pieces = [lax.ppermute(group, "section", route) for group in weights for route in routes]
    near = []
    for k in range(micro_count):
        part = lax.dynamic_index_in_dim(both, (place // replicas) ^ k, 0, keepdims=False)
        near.append(part if k == 0 else exchange(part, k * replicas))
    near = jnp.stack(near)
    fields = [near] + [exchange(near, r) for r in range(1, replicas)]
    fields = [x.reshape(-1, x.shape[-1]) for x in fields]

    def plan(section, place, field):
        first = weights.shape[0] * (sections - 1)
        weight_steps = [
            [
                (group * (sections - 1) + d - 1, 0, weights.shape[1] // 64, lax.rem(section + sections - d, sections), 0, (0,))
                for d in range(1, sections)
            ]
            for group in range(weights.shape[0])
        ]
        plane_steps = [
            (first + r, (2 * k + field) * plane_rows, plane_rows, k * replicas + r)
            for k in range(micro_count)
            for r in range(replicas)
        ]
        return weight_steps, plane_steps

    return pieces + fields, plan


def per_device(inputs, cotangent, conv_weight, mix_weight):
    micro_count, channels, extent_x, extent_y, extent_z = inputs.shape
    groups, _, hidden, taps = conv_weight.shape
    sections = lax.axis_size("section")
    space = lax.axis_size("space")
    section = lax.axis_index("section")
    place = lax.axis_index("space")
    replicas = space // micro_count
    width = taps + channels
    layers = groups * sections
    cells = extent_x * space * extent_z
    lanes = extent_y * channels
    paired = space == 8 and replicas == 2 and sections == 4 and extent_x == 1 and extent_z == 128 and lanes == 128
    me = jnp.stack([section, place, place % replicas]).astype(jnp.int32)

    conv_rows = jnp.swapaxes(conv_weight, 2, 3)
    weights = jnp.concatenate([conv_rows[:, 0], mix_weight[:, 0]], axis=1)
    if paired:
        fields = [x.reshape(micro_count, lanes, extent_z) for x in (inputs, cotangent)]
        pieces, plan = gather_paired(weights, fields, me, place)
    else:
        both = jnp.stack([inputs, cotangent], axis=1)
        both = both.transpose(0, 1, 3, 5, 4, 2).reshape(micro_count, 2, extent_x * extent_z, lanes)
        pieces, plan = gather_plain(weights, both, place, replicas)

    total_x = extent_x * space
    act = jax.ShapeDtypeStruct((cells, lanes), F32)
    kept = [
        jax.ShapeDtypeStruct((sections, 10 * lanes, 2 * hidden), BF),
        jax.ShapeDtypeStruct((sections, cells, 2 * hidden), BF),
        jax.ShapeDtypeStruct((2, total_x + 2, extent_z, 3 * lanes), BF),
        jax.ShapeDtypeStruct((2, cells, 2 * hidden), BF),
    ]
    early = [pieces[i] for i in needed(plan, 0, 0)]
    act, *saved = call(
        functools.partial(first_kernel, plan, len(early)),
        [act] + kept,
        [], 30 * MIB,
        me, conv_rows, mix_weight, *early,
    )
    if paired:
        pieces[7] = exchange(after(pieces[5], act), 1)
    late = [pieces[i] for i in needed(plan, 1, 1)]
    terms = jax.ShapeDtypeStruct((width // replicas, hidden), BF)
    wide = pltpu.VMEM((total_x + 2, extent_z, 9 * lanes), F32)
    whole = pltpu.VMEM((width, hidden), BF)
    up, late_terms = call(
        functools.partial(second_kernel, plan, len(late)),
        [act, terms],
        [pltpu.VMEM(x.shape, x.dtype) for x in kept] + [pltpu.VMEM((cells, lanes), F32), wide, whole],
        40 * MIB,
        me, conv_rows, mix_weight, *late, act,
    )
    traded = cross(late_terms, 2, 4) if paired else None
    (early_terms,) = call(
        functools.partial(third_kernel),
        [terms],
        [pltpu.VMEM((cells, lanes), F32), wide, whole],
        20 * MIB,
        me, up, *saved,
    )

    factor = 1.0 / math.sqrt(micro_count * cells * extent_y)
    outs = [
        jax.ShapeDtypeStruct((groups, 1, taps, hidden), F32),
        jax.ShapeDtypeStruct((groups, 1, channels, hidden), F32),
    ]
    scratch = [pltpu.VMEM((width, hidden), F32), pltpu.SemaphoreType.DMA((3,))]
    grads = ()
    for group in (1, 0):
        own = late_terms if group else early_terms
        if paired:
            met = after(traded, early_terms) if group else cross(own, 2, 4)
            half = (own.astype(F32) + met.astype(F32)).astype(BF)
            other = cross(half, 4, 2)
            kernel, parts = pair_kernel, (half, other, exchange(half, 1), exchange(other, 1))
        else:
            level = [own] + [exchange(own, k * replicas) for k in range(1, micro_count)]
            level = [x.astype(F32) for x in level]
            while len(level) > 1:
                level = [level[i] + level[i + 1] for i in range(0, len(level), 2)]
            rows_of = [[m * replicas + r for r in range(replicas)] for m in range(micro_count)]
            every = lax.all_gather(level[0].astype(BF), "space", axis=0, tiled=True, axis_index_groups=rows_of)
            kernel, parts = plain_kernel, (every,)
        grads = call(functools.partial(kernel, group, factor), outs, scratch, MIB // 16, me, *parts, into=grads)
    conv, mix = grads
    return (jnp.swapaxes(conv, 2, 3), mix)


def solution(mesh):
    placed = (
        P(None, None, "space", None, None),
        P(None, None, "space", None, None),
        P(None, "section", None, None),
        P(None, "section", None, None),
    )
    return jax.shard_map(
        per_device,
        mesh=mesh,
        in_specs=placed,
        out_specs=(P(None, "section", None, None), P(None, "section", None, None)),
        check_vma=False,
    )
```

```python
import functools
import math

import jax
import jax.numpy as jnp
from jax import lax
from jax.experimental import pallas as pl
from jax.experimental.pallas import tpu as pltpu
from jax.sharding import PartitionSpec as P

BF = jnp.bfloat16
F32 = jnp.float32
NT = (((1,), (1,)), ((), ()))
NN = (((1,), (0,)), ((), ()))
TN = (((0,), (0,)), ((), ()))
MIB = 1024 * 1024
SHARES = (
    (0, 3, 6, 1, 4, 7, 2, 5, 8, 9, 12, 15, 10, 13),
    (16, 11, 14, 17, 18, 21, 24, 19, 22, 25, 20, 23, 26, 27),
)


def dot(a, b, dims):
    return lax.dot_general(a, b, dims, preferred_element_type=F32)


def shifted(x, step, length):
    place = lax.broadcasted_iota(jnp.int32, x.shape, 0) % length
    edge = 0 if step > 0 else length - 1
    return jnp.where(place == edge, 0.0, pltpu.roll(x, step % x.shape[0], 0))


def fold_taps(source, start, first, count, layer, folded):
    for tap in range(first, first + count):
        row = start + 64 * (tap - first)
        block = source[row : row + 64]
        if tap == 27:
            at, places = 1152, [(0, 0), (1, 1)]
            for y, other in ((0, 1), (1, 0)):
                folded[layer, at + 64 * y : at + 64 * y + 64, 128 * other : 128 * other + 128] = jnp.zeros_like(block)
        else:
            at = 128 * (3 * (tap // 9) + tap % 3)
            places = [[(0, 1)], [(0, 0), (1, 1)], [(1, 0)]][tap // 3 % 3]
        for y, other in places:
            folded[layer, at + 64 * y : at + 64 * y + 64, 128 * other : 128 * other + 128] = block


def columns_of(padded):
    planes = padded.shape[0] - 2
    parts = [padded[d : d + planes] for d in range(3)]
    return jnp.concatenate(parts, axis=2).reshape(planes * padded.shape[1], 3 * padded.shape[2])


def forward_layer(layer, slot, act, folded, slope, keep_a, keep_h):
    padded = keep_a.at[slot]
    planes = padded.shape[0] - 2
    length = padded.shape[1]
    now = act[...]
    for at, value in enumerate((shifted(now, 1, length), now, shifted(now, -1, length))):
        padded[1 : planes + 1, :, 128 * at : 128 * at + 128] = value.astype(BF).reshape(planes, length, 128)
    pre = dot(columns_of(padded), folded[layer, :1152], NN)
    gate = 0.5 * jnp.tanh(0.5 * pre) + 0.5
    wide = pre * gate
    hidden = wide.astype(BF)
    slope[layer] = (gate + wide * (1.0 - gate)).astype(slope.dtype)
    act[...] = now + dot(hidden, folded[layer, 1152:], NT)
    keep_h[slot] = hidden


def term_rows(blocks, base, conv, mix, terms):
    for number, tap in enumerate(blocks):
        at = 128 * (3 * (tap // 9) + tap % 3 - base)
        if tap == 27:
            value = mix[:64, :128] + mix[64:, 128:]
        elif tap // 3 % 3 == 1:
            value = conv[at : at + 64, :128] + conv[at + 64 : at + 128, 128:]
        elif tap // 3 % 3 == 0:
            value = conv[at : at + 64, 128:]
        else:
            value = conv[at + 64 : at + 128, :128]
        terms[64 * number : 64 * number + 64] = value.astype(BF)


def some_columns(padded, groups):
    planes = padded.shape[0] - 2
    parts = []
    for d in range(3):
        inside = [g - 3 * d for g in groups if g // 3 == d]
        if inside:
            parts.append(padded[d : d + planes, :, 128 * inside[0] : 128 * inside[-1] + 128])
    return jnp.concatenate(parts, axis=2).reshape(planes * padded.shape[1], 128 * len(groups))


def backward_layer(shares, mine, layer, owned, up, grad, wide, folded, slope, keep_a, keep_h, terms, spread_if):
    planes = wide.shape[0] - 2
    length = wide.shape[1]
    now = up[...]
    half = now.shape[0] // 2
    for rows in (slice(0, half), slice(half, 2 * half)):
        hid_grad = dot(now[rows].astype(BF), folded[layer, 1152:], NN)
        grad[rows] = (hid_grad * slope[layer, rows]).astype(BF)

    for replica, blocks in enumerate(shares):
        groups = sorted({3 * (tap // 9) + tap % 3 for tap in blocks if tap < 27})

        @pl.when(owned & (mine == replica) if len(shares) > 1 else owned)
        def _(blocks=blocks, groups=groups):
            conv = dot(some_columns(keep_a.at[0], groups), grad[...], TN)
            mix = dot(up[...].astype(BF), keep_h[0], TN) if 27 in blocks else None
            term_rows(blocks, groups[0], conv, mix, terms)

    def spread():
        wide[1 : planes + 1] = dot(grad[...], folded[layer, :1152], NT).reshape(planes, length, 1152)
        total = up[...]
        for dz in range(3):
            part = 0.0
            for dx in range(3):
                at = 128 * (3 * dx + dz)
                part = part + wide[2 - dx : 2 - dx + planes, :, at : at + 128]
            part = part.reshape(planes * length, 128)
            total = total + (part if dz == 1 else shifted(part, dz - 1, length))
        up[...] = total

    if spread_if is None:
        spread()
    else:
        pl.when(spread_if)(spread)


def clear_edges(ref):
    ref[0] = jnp.zeros(ref.shape[1:], ref.dtype)
    ref[ref.shape[0] - 1] = jnp.zeros(ref.shape[1:], ref.dtype)


def needed(plan, group, field):
    weight_steps, plane_steps = plan(0, 0, field)
    return sorted({step[0] for step in weight_steps[group] + plane_steps})


def take(plan, me_ref, field, group, conv, mix, pieces, folded, target):
    section, place = me_ref[0], me_ref[1]
    taps = conv.shape[2] // 64
    fold_taps(conv.at[group, 0], 0, 0, taps, section, folded)
    fold_taps(mix.at[group, 0], 0, taps, 1, section, folded)
    weight_steps, plane_steps = plan(section, place, field)
    pieces = dict(zip(needed(plan, group, field), pieces, strict=True))
    for piece, start, count, layer, first, choices in weight_steps[group]:
        for choice in choices:

            @pl.when(first == choice)
            def _(piece=piece, start=start, count=count, layer=layer, choice=choice):
                fold_taps(pieces[piece], start, choice, count, layer, folded)

    for piece, start, rows, rel in plane_steps:
        row = pl.multiple_of((place ^ rel) * rows, rows)
        target[pl.ds(row, rows)] = pieces[piece][start : start + rows].astype(F32)


def begin(copies, sems, first):
    started = []
    for number, (source, target) in enumerate(copies):
        copy = pltpu.make_async_copy(source, target, sems.at[first + number])
        copy.start()
        started.append(copy)
    return started


def finish(started):
    for copy in started:
        copy.wait()


def split_kernel(me_ref, inputs, cotangent, token, own, beside, across, swap):
    chip, core = me_ref[1] // 2, me_ref[1] % 2
    old = lax.broadcasted_iota(jnp.int32, (128, 128), 0)
    new = lax.broadcasted_iota(jnp.int32, (128, 128), 1)
    order = ((old % 2) * 64 + old // 2 == new).astype(F32).astype(BF)
    for number, source in enumerate((inputs, cotangent)):
        rows = slice(128 * number, 128 * number + 128)

        def turned(offset, source=source):
            return dot(source[chip ^ offset], order, TN).astype(BF)

        mine, far = turned(0), turned(3)
        one, two = turned(1 + core), turned(2 - core)
        own[rows] = mine
        across[rows] = far
        beside[rows] = one
        swap[rows] = mine
        swap[256 + 128 * number : 384 + 128 * number] = two


def first_kernel(plan, piece_count, me_ref, conv, mix, *refs):
    pieces, refs = refs[:piece_count], refs[piece_count:]
    act, folded, slope, keep_a, keep_h = refs
    section = me_ref[0]
    take(plan, me_ref, 0, 0, conv, mix, pieces, folded, act)
    for slot in range(2):
        clear_edges(keep_a.at[slot])

    def step(layer, carry):
        forward_layer(layer, jnp.where(layer == section, 0, 1), act, folded, slope, keep_a, keep_h)
        return carry

    lax.fori_loop(0, folded.shape[0], step, 0)


def all_back(shares, me_ref, last, up, grad, wide, folded, slope, keep_a, keep_h, terms, out):
    section, replica = me_ref[0], me_ref[2]
    sections = folded.shape[0]
    target = out if len(shares) > 1 else terms

    def back(i, carry):
        layer = sections - 1 - i
        spread_if = None if last else layer > 0
        backward_layer(
            shares, replica, layer, layer == section, up, grad, wide, folded, slope, keep_a, keep_h, target, spread_if
        )
        return carry

    lax.fori_loop(0, sections, back, 0)
    if len(shares) == 1:
        rows = out.shape[0]
        out[...] = terms[pl.ds(pl.multiple_of(replica * rows, rows), rows)]


def second_kernel(shares, plan, piece_count, me_ref, conv, mix, *refs):
    pieces, refs = refs[:piece_count], refs[piece_count:]
    act_in, up, out, folded, slope, keep_a, keep_h, act, wide, terms, grad = refs
    section = me_ref[0]
    act[...] = act_in[...]
    take(plan, me_ref, 1, 1, conv, mix, pieces, folded, up)
    for slot in range(2):
        clear_edges(keep_a.at[slot])
    clear_edges(wide)

    def step(layer, carry):
        forward_layer(layer, jnp.where(layer == section, 0, 1), act, folded, slope, keep_a, keep_h)
        return carry

    lax.fori_loop(0, folded.shape[0], step, 0)
    all_back(shares, me_ref, True, up, grad, wide, folded, slope, keep_a, keep_h, terms, out)


def third_kernel(shares, me_ref, up_in, folded, slope, keep_a, keep_h, out, up, wide, terms, grad):
    up[...] = up_in[...]
    clear_edges(wide)
    all_back(shares, me_ref, False, up, grad, wide, folded, slope, keep_a, keep_h, terms, out)


def send_taps(taps, factor, value, conv, mix, group, whole, sems):
    for number, tap in enumerate(taps):
        whole[64 * tap : 64 * tap + 64] = value[64 * number : 64 * number + 64] * factor
    runs = []
    for tap in sorted(taps):
        if runs and tap < 27 and tap == runs[-1][1]:
            runs[-1][1] += 1
        else:
            runs.append([tap, tap + 1])
    copies = []
    for start, stop in runs:
        rows = pl.ds(64 * start, 64 * (stop - start))
        copies.append((whole.at[rows], mix.at[group, 0] if start == 27 else conv.at[group, 0, rows]))
    return begin(copies, sems, 0)


def pair_kernel(group, factor, swapped, me_ref, a, b, *refs):
    conv, mix, whole, sems = refs[-4:]
    for core in range(2):

        @pl.when((me_ref[2] ^ swapped) == core)
        def _(core=core):
            value = a[...].astype(F32) + b[...].astype(F32)
            finish(send_taps(SHARES[core], factor, value, conv, mix, group, whole, sems))


def both_kernel(group, factor, me_ref, own_a, own_b, far_a, far_b, *refs):
    conv, mix, whole, sems = refs[-4:]
    first = me_ref[2] == 0
    own = own_a[...].astype(F32) + own_b[...].astype(F32)
    far = far_a[...].astype(F32) + far_b[...].astype(F32)
    started = send_taps(SHARES[0], factor, jnp.where(first, own, far), conv, mix, group, whole, sems.at[0])
    started += send_taps(SHARES[1], factor, jnp.where(first, far, own), conv, mix, group, whole, sems.at[1])
    finish(started)


def plain_kernel(group, factor, me_ref, terms, *refs):
    conv, mix, whole, sems = refs[-4:]
    finish(send_taps(range(28), factor, terms[...].astype(F32), conv, mix, group, whole, sems.at[0]))


def size_of(x):
    return math.prod(x.shape) * x.dtype.itemsize


def call(kernel, outs, scratch, traffic, *args, into=()):
    vmem = pl.BlockSpec(memory_space=pltpu.VMEM)
    far = pl.BlockSpec(memory_space=pl.ANY)
    specs = [pl.BlockSpec(memory_space=pltpu.SMEM)] + [vmem] * (len(args) - 1) + [far] * len(into)
    held = sum(size_of(x) for x in scratch if x.memory_space == pltpu.VMEM)
    passed = sum(size_of(x) for x in args) + sum(size_of(x) for x in outs)
    limit = held + held // 4 + 10 * MIB
    if held + passed > 30 * MIB:
        limit = 63 * MIB
    return pl.pallas_call(
        kernel,
        out_shape=outs,
        in_specs=specs,
        out_specs=[far if kernel.func in (pair_kernel, both_kernel, plain_kernel) else vmem] * len(outs),
        scratch_shapes=scratch,
        input_output_aliases={len(args) + i: i for i in range(len(into))},
        compiler_params=pltpu.CompilerParams(vmem_limit_bytes=limit),
        cost_estimate=pl.CostEstimate(flops=traffic * 100, bytes_accessed=traffic, transcendentals=0),
    )(*args, *into)


def exchange(block, mask):
    count = lax.axis_size("space")
    return lax.ppermute(block, "space", [(i, i ^ mask) for i in range(count)])


def cross(block, first, second):
    count = lax.axis_size("space")
    return lax.ppermute(block, "space", [(i, i ^ (second if i % 2 else first)) for i in range(count)])


def after(x, *others):
    return lax.optimization_barrier((x, *others))[0]


def gather_paired(weights, fields, me, place):
    sections, space = lax.axis_size("section"), lax.axis_size("space")
    rows = weights.shape[1]
    half, quarter = rows // 2, rows // 4
    chip, core = place // 2, place % 2
    side = (chip // 2) ^ (chip % 2)
    mine = jnp.where(side == 0, weights[:, :half], weights[:, half:])
    part = lax.dynamic_slice_in_dim(mine, core * quarter, quarter, axis=1)
    route = []
    for s in range(sections):
        for j in range(space):
            target = (s + (-1 if j % 2 else 1)) % sections
            route.append((s * space + j, target * space + j))
    across = [(s, (s + 2) % sections) for s in range(sections)]
    token = exchange(mine[0, :16], 1)
    own, beside, diagonal, swap = call(
        functools.partial(split_kernel),
        [jax.ShapeDtypeStruct((count, 128), BF) for count in (256, 256, 256, 512)],
        [], MIB, me, *fields, token,
    )
    other = exchange(swap, 1)
    diagonal = exchange(diagonal, 6)
    near, far = [], []
    for group in range(2):
        near.append(lax.ppermute(after(mine[group], *near), ("section", "space"), route))
        far.append(lax.ppermute(after(part[group], *near[:group]), "section", across))
    sent = [beside, other[256:]]
    diagonal_far = exchange(diagonal, 1)
    pieces = []
    for group in range(2):
        here = jnp.concatenate([near[group], far[group]] + (sent if group == 0 else []), axis=0)
        there = cross(here, 2, 4)
        pieces += [here, there, exchange(here, 1), None if group else exchange(after(there, diagonal, near[1], far[1]), 1)]
    planes = [own, other, diagonal, diagonal_far]
    plane_rows = 128

    def plan(section, place, field):
        chip, core = place // 2, place % 2
        side = (chip // 2) ^ (chip % 2)
        weight_steps = []
        for group in range(2):
            steps = []
            for swapped in range(2):
                source = core ^ swapped
                beside = lax.rem(section + sections - 1 + 2 * source, sections)
                across = lax.rem(section + 2, sections)
                for other in range(2):
                    piece = 4 * group + 2 * swapped + other
                    first = (side ^ other) * 14
                    steps.append((piece, 0, 14, beside, first, (0, 14)))
                    steps.append((piece, half, 7, across, first + source * 7, (0, 7, 14, 21)))
            weight_steps.append(steps)
        plane_steps = []
        start = field * plane_rows
        for piece, rel in ((8, 0), (9, 1), (10, 6), (11, 7)):
            plane_steps.append((piece, start, plane_rows, rel))
        for swapped in range(2):
            rel = swapped ^ (2 + 2 * (core ^ swapped))
            start = half + quarter + field * plane_rows
            plane_steps.append((1 + 2 * swapped, start, plane_rows, rel))
            plane_steps.append((1 + 2 * swapped, start + 2 * plane_rows, plane_rows, rel ^ 1))
        return weight_steps, plane_steps

    return pieces + planes, plan


def gather_plain(weights, both, place, replicas):
    sections = lax.axis_size("section")
    micro_count, _, plane_rows, _ = both.shape
    routes = [[(i, (i + d) % sections) for i in range(sections)] for d in range(1, sections)]
    pieces = [lax.ppermute(group, "section", route) for group in weights for route in routes]
    near = []
    for k in range(micro_count):
        part = lax.dynamic_index_in_dim(both, (place // replicas) ^ k, 0, keepdims=False)
        near.append(part if k == 0 else exchange(part, k * replicas))
    near = jnp.stack(near)
    fields = [near] + [exchange(near, r) for r in range(1, replicas)]
    fields = [x.reshape(-1, x.shape[-1]) for x in fields]

    def plan(section, place, field):
        first = weights.shape[0] * (sections - 1)
        weight_steps = [
            [
                (group * (sections - 1) + d - 1, 0, weights.shape[1] // 64, lax.rem(section + sections - d, sections), 0, (0,))
                for d in range(1, sections)
            ]
            for group in range(weights.shape[0])
        ]
        plane_steps = [
            (first + r, (2 * k + field) * plane_rows, plane_rows, k * replicas + r)
            for k in range(micro_count)
            for r in range(replicas)
        ]
        return weight_steps, plane_steps

    return pieces + fields, plan


def per_device(inputs, cotangent, conv_weight, mix_weight):
    micro_count, channels, extent_x, extent_y, extent_z = inputs.shape
    groups, _, hidden, taps = conv_weight.shape
    sections = lax.axis_size("section")
    space = lax.axis_size("space")
    section = lax.axis_index("section")
    place = lax.axis_index("space")
    replicas = space // micro_count
    width = taps + channels
    layers = groups * sections
    cells = extent_x * space * extent_z
    lanes = extent_y * channels
    paired = space == 8 and replicas == 2 and sections == 4 and extent_x == 1 and extent_z == 128 and lanes == 128
    me = jnp.stack([section, place, place % replicas]).astype(jnp.int32)

    conv_rows = jnp.swapaxes(conv_weight, 2, 3)
    weights = jnp.concatenate([conv_rows[:, 0], mix_weight[:, 0]], axis=1)
    if paired:
        fields = [x.reshape(micro_count, lanes, extent_z) for x in (inputs, cotangent)]
        pieces, plan = gather_paired(weights, fields, me, place)
    else:
        both = jnp.stack([inputs, cotangent], axis=1)
        both = both.transpose(0, 1, 3, 5, 4, 2).reshape(micro_count, 2, extent_x * extent_z, lanes)
        pieces, plan = gather_plain(weights, both, place, replicas)

    total_x = extent_x * space
    act = jax.ShapeDtypeStruct((cells, lanes), F32)
    kept = [
        jax.ShapeDtypeStruct((sections, 10 * lanes, 2 * hidden), BF),
        jax.ShapeDtypeStruct((sections, cells, 2 * hidden), BF),
        jax.ShapeDtypeStruct((2, total_x + 2, extent_z, 3 * lanes), BF),
        jax.ShapeDtypeStruct((2, cells, 2 * hidden), BF),
    ]
    early = [pieces[i] for i in needed(plan, 0, 0)]
    act, *saved = call(
        functools.partial(first_kernel, plan, len(early)),
        [act] + kept,
        [], 30 * MIB,
        me, conv_rows, mix_weight, *early,
    )
    if paired:
        pieces[7] = exchange(after(pieces[5], act), 1)
    late = [pieces[i] for i in needed(plan, 1, 1)]
    terms = jax.ShapeDtypeStruct((width // replicas, hidden), BF)
    shares = SHARES if paired else (tuple(range(28)),)
    wide = pltpu.VMEM((total_x + 2, extent_z, 9 * lanes), F32)
    whole = pltpu.VMEM((width, hidden), BF)
    grad = pltpu.VMEM((cells, 2 * hidden), BF)
    up, late_terms = call(
        functools.partial(second_kernel, shares, plan, len(late)),
        [act, terms],
        [pltpu.VMEM(x.shape, x.dtype) for x in kept] + [pltpu.VMEM((cells, lanes), F32), wide, whole, grad],
        40 * MIB,
        me, conv_rows, mix_weight, *late, act,
    )
    traded = cross(late_terms, 2, 4) if paired else None
    (early_terms,) = call(
        functools.partial(third_kernel, shares),
        [terms],
        [pltpu.VMEM((cells, lanes), F32), wide, whole, grad],
        20 * MIB,
        me, up, *saved,
    )

    factor = 1.0 / math.sqrt(micro_count * cells * extent_y)
    outs = [
        jax.ShapeDtypeStruct((groups, 1, taps, hidden), F32),
        jax.ShapeDtypeStruct((groups, 1, channels, hidden), F32),
    ]
    scratch = [pltpu.VMEM((width, hidden), F32), pltpu.SemaphoreType.DMA((2, 8))]
    grads = ()
    for group in (1, 0):
        own = late_terms if group else early_terms
        if paired:
            met = after(traded, early_terms) if group else cross(own, 2, 4)
            half = (own.astype(F32) + met.astype(F32)).astype(BF)
            other = cross(half, 4, 2)
            kernel, parts = both_kernel, (half, other, exchange(half, 1), exchange(other, 1))
        else:
            level = [own] + [exchange(own, k * replicas) for k in range(1, micro_count)]
            level = [x.astype(F32) for x in level]
            while len(level) > 1:
                level = [level[i] + level[i + 1] for i in range(0, len(level), 2)]
            rows_of = [[m * replicas + r for r in range(replicas)] for m in range(micro_count)]
            every = lax.all_gather(level[0].astype(BF), "space", axis=0, tiled=True, axis_index_groups=rows_of)
            kernel, parts = plain_kernel, (every,)
        grads = call(functools.partial(kernel, group, factor), outs, scratch, MIB // 16, me, *parts, into=grads)
    conv, mix = grads
    return (jnp.swapaxes(conv, 2, 3), mix)


def solution(mesh):
    placed = (
        P(None, None, "space", None, None),
        P(None, None, "space", None, None),
        P(None, "section", None, None),
        P(None, "section", None, None),
    )
    return jax.shard_map(
        per_device,
        mesh=mesh,
        in_specs=placed,
        out_specs=(P(None, "section", None, None), P(None, "section", None, None)),
        check_vma=False,
    )
```

```python
import functools
import math

import jax
import jax.numpy as jnp
from jax import lax
from jax.experimental import pallas as pl
from jax.experimental.pallas import tpu as pltpu
from jax.sharding import PartitionSpec as P

BF = jnp.bfloat16
F32 = jnp.float32
NT = (((1,), (1,)), ((), ()))
NN = (((1,), (0,)), ((), ()))
TN = (((0,), (0,)), ((), ()))
MIB = 1024 * 1024
SHARES = (
    (0, 3, 6, 1, 4, 7, 2, 5, 8, 9, 12, 15, 10, 13),
    (16, 11, 14, 17, 18, 21, 24, 19, 22, 25, 20, 23, 26, 27),
)


def dot(a, b, dims):
    return lax.dot_general(a, b, dims, preferred_element_type=F32)


def shifted(x, step, length):
    place = lax.broadcasted_iota(jnp.int32, x.shape, 0) % length
    edge = 0 if step > 0 else length - 1
    return jnp.where(place == edge, 0.0, pltpu.roll(x, step % x.shape[0], 0))


def fold_taps(source, start, first, count, layer, folded):
    for tap in range(first, first + count):
        row = start + 64 * (tap - first)
        block = source[row : row + 64]
        if tap == 27:
            at, places = 1152, [(0, 0), (1, 1)]
            for y, other in ((0, 1), (1, 0)):
                folded[layer, at + 64 * y : at + 64 * y + 64, 128 * other : 128 * other + 128] = jnp.zeros_like(block)
        else:
            at = 128 * (3 * (tap // 9) + tap % 3)
            places = [[(0, 1)], [(0, 0), (1, 1)], [(1, 0)]][tap // 3 % 3]
        for y, other in places:
            folded[layer, at + 64 * y : at + 64 * y + 64, 128 * other : 128 * other + 128] = block


def columns_of(padded):
    planes = padded.shape[0] - 2
    parts = [padded[d : d + planes] for d in range(3)]
    return jnp.concatenate(parts, axis=2).reshape(planes * padded.shape[1], 3 * padded.shape[2])


def forward_layer(layer, slot, act, folded, slope, keep_a, keep_h):
    padded = keep_a.at[slot]
    planes = padded.shape[0] - 2
    length = padded.shape[1]
    now = act[...]
    for at, value in enumerate((shifted(now, 1, length), now, shifted(now, -1, length))):
        padded[1 : planes + 1, :, 128 * at : 128 * at + 128] = value.astype(BF).reshape(planes, length, 128)
    pre = dot(columns_of(padded), folded[layer, :1152], NN)
    gate = 0.5 * jnp.tanh(0.5 * pre) + 0.5
    wide = pre * gate
    hidden = wide.astype(BF)
    slope[layer] = (gate + wide * (1.0 - gate)).astype(slope.dtype)
    act[...] = now + dot(hidden, folded[layer, 1152:], NT)
    keep_h[slot] = hidden


def term_rows(blocks, base, conv, mix, terms):
    for number, tap in enumerate(blocks):
        at = 128 * (3 * (tap // 9) + tap % 3 - base)
        if tap == 27:
            value = mix[:64, :128] + mix[64:, 128:]
        elif tap // 3 % 3 == 1:
            value = conv[at : at + 64, :128] + conv[at + 64 : at + 128, 128:]
        elif tap // 3 % 3 == 0:
            value = conv[at : at + 64, 128:]
        else:
            value = conv[at + 64 : at + 128, :128]
        terms[64 * number : 64 * number + 64] = value.astype(BF)


def some_columns(padded, groups):
    planes = padded.shape[0] - 2
    parts = []
    for d in range(3):
        inside = [g - 3 * d for g in groups if g // 3 == d]
        if inside:
            parts.append(padded[d : d + planes, :, 128 * inside[0] : 128 * inside[-1] + 128])
    return jnp.concatenate(parts, axis=2).reshape(planes * padded.shape[1], 128 * len(groups))


def backward_layer(shares, mine, layer, owned, up, grad, wide, folded, slope, keep_a, keep_h, terms, spread_if):
    planes = wide.shape[0] - 2
    length = wide.shape[1]
    now = up[...]
    half = now.shape[0] // 2
    for rows in (slice(0, half), slice(half, 2 * half)):
        hid_grad = dot(now[rows].astype(BF), folded[layer, 1152:], NN)
        grad[rows] = (hid_grad * slope[layer, rows]).astype(BF)

    for replica, blocks in enumerate(shares):
        groups = sorted({3 * (tap // 9) + tap % 3 for tap in blocks if tap < 27})

        @pl.when(owned & (mine == replica) if len(shares) > 1 else owned)
        def _(blocks=blocks, groups=groups):
            conv = dot(some_columns(keep_a.at[0], groups), grad[...], TN)
            mix = dot(up[...].astype(BF), keep_h[0], TN) if 27 in blocks else None
            term_rows(blocks, groups[0], conv, mix, terms)

    def spread():
        wide[1 : planes + 1] = dot(grad[...], folded[layer, :1152], NT).reshape(planes, length, 1152)
        total = up[...]
        for dz in range(3):
            part = 0.0
            for dx in range(3):
                at = 128 * (3 * dx + dz)
                part = part + wide[2 - dx : 2 - dx + planes, :, at : at + 128]
            part = part.reshape(planes * length, 128)
            total = total + (part if dz == 1 else shifted(part, dz - 1, length))
        up[...] = total

    if spread_if is None:
        spread()
    else:
        pl.when(spread_if)(spread)


def clear_edges(ref):
    ref[0] = jnp.zeros(ref.shape[1:], ref.dtype)
    ref[ref.shape[0] - 1] = jnp.zeros(ref.shape[1:], ref.dtype)


def needed(plan, group, field):
    weight_steps, plane_steps = plan(0, 0, field)
    return sorted({step[0] for step in weight_steps[group] + plane_steps})


def take(plan, me_ref, field, group, conv, mix, pieces, folded, target):
    section, place = me_ref[0], me_ref[1]
    taps = conv.shape[2] // 64
    fold_taps(conv.at[group, 0], 0, 0, taps, section, folded)
    fold_taps(mix.at[group, 0], 0, taps, 1, section, folded)
    weight_steps, plane_steps = plan(section, place, field)
    pieces = dict(zip(needed(plan, group, field), pieces, strict=True))
    for piece, start, count, layer, first, choices in weight_steps[group]:
        for choice in choices:

            @pl.when(first == choice)
            def _(piece=piece, start=start, count=count, layer=layer, choice=choice):
                fold_taps(pieces[piece], start, choice, count, layer, folded)

    for piece, start, rows, rel in plane_steps:
        row = pl.multiple_of((place ^ rel) * rows, rows)
        target[pl.ds(row, rows)] = pieces[piece][start : start + rows].astype(F32)


def begin(copies, sems, first):
    started = []
    for number, (source, target) in enumerate(copies):
        copy = pltpu.make_async_copy(source, target, sems.at[first + number])
        copy.start()
        started.append(copy)
    return started


def finish(started):
    for copy in started:
        copy.wait()


def split_kernel(me_ref, inputs, cotangent, token, own, beside, across, swap):
    chip, core = me_ref[1] // 2, me_ref[1] % 2
    old = lax.broadcasted_iota(jnp.int32, (128, 128), 0)
    new = lax.broadcasted_iota(jnp.int32, (128, 128), 1)
    order = ((old % 2) * 64 + old // 2 == new).astype(F32).astype(BF)
    for number, source in enumerate((inputs, cotangent)):
        rows = slice(128 * number, 128 * number + 128)

        def turned(offset, source=source):
            return dot(source[chip ^ offset], order, TN).astype(BF)

        mine, far = turned(0), turned(3)
        one, two = turned(1 + core), turned(2 - core)
        own[rows] = mine
        across[rows] = far
        beside[rows] = one
        swap[rows] = mine
        swap[256 + 128 * number : 384 + 128 * number] = two


def first_kernel(plan, piece_count, me_ref, conv, mix, *refs):
    pieces, refs = refs[:piece_count], refs[piece_count:]
    act, folded, slope, keep_a, keep_h, mark = refs
    section = me_ref[0]
    take(plan, me_ref, 0, 0, conv, mix, pieces, folded, act)
    for slot in range(2):
        clear_edges(keep_a.at[slot])
    mark[...] = jnp.zeros_like(mark)

    def step(layer, carry):
        forward_layer(layer, jnp.where(layer == section, 0, 1), act, folded, slope, keep_a, keep_h)
        return carry

    lax.fori_loop(0, folded.shape[0] - 1, step, 0)


def next_kernel(me_ref, mark, folded, *refs):
    act, slope, keep_a, keep_h = refs[-4:]
    layer = folded.shape[0] - 1
    forward_layer(layer, jnp.where(layer == me_ref[0], 0, 1), act, folded, slope, keep_a, keep_h)


def all_back(shares, me_ref, last, up, grad, wide, folded, slope, keep_a, keep_h, terms, out):
    section, replica = me_ref[0], me_ref[2]
    sections = folded.shape[0]
    target = out if len(shares) > 1 else terms

    def back(i, carry):
        layer = sections - 1 - i
        spread_if = None if last else layer > 0
        backward_layer(
            shares, replica, layer, layer == section, up, grad, wide, folded, slope, keep_a, keep_h, target, spread_if
        )
        return carry

    lax.fori_loop(0, sections, back, 0)
    if len(shares) == 1:
        rows = out.shape[0]
        out[...] = terms[pl.ds(pl.multiple_of(replica * rows, rows), rows)]


def second_kernel(shares, plan, piece_count, me_ref, conv, mix, *refs):
    pieces, refs = refs[:piece_count], refs[piece_count:]
    act_in, up, out, folded, slope, keep_a, keep_h, act, wide, terms, grad = refs
    section = me_ref[0]
    act[...] = act_in[...]
    take(plan, me_ref, 1, 1, conv, mix, pieces, folded, up)
    for slot in range(2):
        clear_edges(keep_a.at[slot])
    clear_edges(wide)

    def step(layer, carry):
        forward_layer(layer, jnp.where(layer == section, 0, 1), act, folded, slope, keep_a, keep_h)
        return carry

    lax.fori_loop(0, folded.shape[0], step, 0)
    all_back(shares, me_ref, True, up, grad, wide, folded, slope, keep_a, keep_h, terms, out)


def third_kernel(shares, me_ref, up_in, folded, slope, keep_a, keep_h, out, up, wide, terms, grad):
    up[...] = up_in[...]
    clear_edges(wide)
    all_back(shares, me_ref, False, up, grad, wide, folded, slope, keep_a, keep_h, terms, out)


def send_taps(taps, factor, value, conv, mix, group, whole, sems):
    for number, tap in enumerate(taps):
        whole[64 * tap : 64 * tap + 64] = value[64 * number : 64 * number + 64] * factor
    runs = []
    for tap in sorted(taps):
        if runs and tap < 27 and tap == runs[-1][1]:
            runs[-1][1] += 1
        else:
            runs.append([tap, tap + 1])
    copies = []
    for start, stop in runs:
        rows = pl.ds(64 * start, 64 * (stop - start))
        copies.append((whole.at[rows], mix.at[group, 0] if start == 27 else conv.at[group, 0, rows]))
    return begin(copies, sems, 0)


def pair_kernel(group, factor, swapped, me_ref, a, b, *refs):
    conv, mix, whole, sems = refs[-4:]
    for core in range(2):

        @pl.when((me_ref[2] ^ swapped) == core)
        def _(core=core):
            value = a[...].astype(F32) + b[...].astype(F32)
            finish(send_taps(SHARES[core], factor, value, conv, mix, group, whole, sems))


def both_kernel(group, factor, me_ref, own_a, own_b, far_a, far_b, *refs):
    conv, mix, whole, sems = refs[-4:]
    first = me_ref[2] == 0
    own = own_a[...].astype(F32) + own_b[...].astype(F32)
    far = far_a[...].astype(F32) + far_b[...].astype(F32)
    started = send_taps(SHARES[0], factor, jnp.where(first, own, far), conv, mix, group, whole, sems.at[0])
    started += send_taps(SHARES[1], factor, jnp.where(first, far, own), conv, mix, group, whole, sems.at[1])
    finish(started)


def plain_kernel(group, factor, me_ref, terms, *refs):
    conv, mix, whole, sems = refs[-4:]
    finish(send_taps(range(28), factor, terms[...].astype(F32), conv, mix, group, whole, sems.at[0]))


def size_of(x):
    return math.prod(x.shape) * x.dtype.itemsize


def call(kernel, outs, scratch, traffic, *args, into=()):
    vmem = pl.BlockSpec(memory_space=pltpu.VMEM)
    far = pl.BlockSpec(memory_space=pl.ANY)
    specs = [pl.BlockSpec(memory_space=pltpu.SMEM)] + [vmem] * (len(args) - 1) + [vmem if kernel.func is next_kernel else far] * len(into)
    held = sum(size_of(x) for x in scratch if x.memory_space == pltpu.VMEM)
    passed = sum(size_of(x) for x in args) + sum(size_of(x) for x in outs)
    limit = held + held // 4 + 10 * MIB
    if held + passed > 30 * MIB:
        limit = 63 * MIB
    return pl.pallas_call(
        kernel,
        out_shape=outs,
        in_specs=specs,
        out_specs=[far if kernel.func in (pair_kernel, both_kernel, plain_kernel) else vmem] * len(outs),
        scratch_shapes=scratch,
        input_output_aliases={len(args) + i: i for i in range(len(into))},
        compiler_params=pltpu.CompilerParams(vmem_limit_bytes=limit),
        cost_estimate=pl.CostEstimate(flops=traffic * 100, bytes_accessed=traffic, transcendentals=0),
    )(*args, *into)


def exchange(block, mask):
    count = lax.axis_size("space")
    return lax.ppermute(block, "space", [(i, i ^ mask) for i in range(count)])


def cross(block, first, second):
    count = lax.axis_size("space")
    return lax.ppermute(block, "space", [(i, i ^ (second if i % 2 else first)) for i in range(count)])


def after(x, *others):
    return lax.optimization_barrier((x, *others))[0]


def gather_paired(weights, fields, me, place):
    sections, space = lax.axis_size("section"), lax.axis_size("space")
    rows = weights.shape[1]
    half, quarter = rows // 2, rows // 4
    chip, core = place // 2, place % 2
    side = (chip // 2) ^ (chip % 2)
    mine = jnp.where(side == 0, weights[:, :half], weights[:, half:])
    part = lax.dynamic_slice_in_dim(mine, core * quarter, quarter, axis=1)
    route = []
    for s in range(sections):
        for j in range(space):
            target = (s + (-1 if j % 2 else 1)) % sections
            route.append((s * space + j, target * space + j))
    across = [(s, (s + 2) % sections) for s in range(sections)]
    token = exchange(mine[0, :16], 1)
    own, beside, diagonal, swap = call(
        functools.partial(split_kernel),
        [jax.ShapeDtypeStruct((count, 128), BF) for count in (256, 256, 256, 512)],
        [], MIB, me, *fields, token,
    )
    other = exchange(swap, 1)
    diagonal = exchange(diagonal, 6)
    near, far = [], []
    for group in range(2):
        near.append(lax.ppermute(after(mine[group], *near), ("section", "space"), route))
        far.append(lax.ppermute(after(part[group], *near[:group]), "section", across))
    sent = [beside, other[256:]]
    diagonal_far = exchange(diagonal, 1)
    here = [jnp.concatenate([near[g], far[g]] + (sent if g == 0 else []), axis=0) for g in range(2)]
    here[0] = after(here[0], diagonal)
    there = [cross(x, 2, 4) for x in here]
    late = exchange(here[1], 1)
    ready = after(there[0], late)
    pieces = [here[0], there[0], exchange(here[0], 1), exchange(ready[:half], 1), here[1], there[1], late, None]
    planes = [own, other, diagonal, diagonal_far, exchange(ready[half:], 1)]
    plane_rows = 128

    def plan(section, place, field):
        chip, core = place // 2, place % 2
        side = (chip // 2) ^ (chip % 2)

        def where(piece, row):
            return (12, row - half) if piece == 3 and row >= half else (piece, row)

        weight_steps = []
        for group in range(2):
            steps = []
            for swapped in range(2):
                source = core ^ swapped
                beside = lax.rem(section + sections - 1 + 2 * source, sections)
                across = lax.rem(section + 2, sections)
                for other in range(2):
                    piece = 4 * group + 2 * swapped + other
                    first = (side ^ other) * 14
                    steps.append((piece, 0, 14, beside, first, (0, 14)))
                    steps.append((*where(piece, half), 7, across, first + source * 7, (0, 7, 14, 21)))
            weight_steps.append(steps)
        plane_steps = []
        start = field * plane_rows
        for piece, rel in ((8, 0), (9, 1), (10, 6), (11, 7)):
            plane_steps.append((piece, start, plane_rows, rel))
        for swapped in range(2):
            rel = swapped ^ (2 + 2 * (core ^ swapped))
            start = half + quarter + field * plane_rows
            plane_steps.append((*where(1 + 2 * swapped, start), plane_rows, rel))
            plane_steps.append((*where(1 + 2 * swapped, start + 2 * plane_rows), plane_rows, rel ^ 1))
        return weight_steps, plane_steps

    return pieces + planes, plan


def gather_plain(weights, both, place, replicas):
    sections = lax.axis_size("section")
    micro_count, _, plane_rows, _ = both.shape
    routes = [[(i, (i + d) % sections) for i in range(sections)] for d in range(1, sections)]
    pieces = [lax.ppermute(group, "section", route) for group in weights for route in routes]
    near = []
    for k in range(micro_count):
        part = lax.dynamic_index_in_dim(both, (place // replicas) ^ k, 0, keepdims=False)
        near.append(part if k == 0 else exchange(part, k * replicas))
    near = jnp.stack(near)
    fields = [near] + [exchange(near, r) for r in range(1, replicas)]
    fields = [x.reshape(-1, x.shape[-1]) for x in fields]

    def plan(section, place, field):
        first = weights.shape[0] * (sections - 1)
        weight_steps = [
            [
                (group * (sections - 1) + d - 1, 0, weights.shape[1] // 64, lax.rem(section + sections - d, sections), 0, (0,))
                for d in range(1, sections)
            ]
            for group in range(weights.shape[0])
        ]
        plane_steps = [
            (first + r, (2 * k + field) * plane_rows, plane_rows, k * replicas + r)
            for k in range(micro_count)
            for r in range(replicas)
        ]
        return weight_steps, plane_steps

    return pieces + fields, plan


def per_device(inputs, cotangent, conv_weight, mix_weight):
    micro_count, channels, extent_x, extent_y, extent_z = inputs.shape
    groups, _, hidden, taps = conv_weight.shape
    sections = lax.axis_size("section")
    space = lax.axis_size("space")
    section = lax.axis_index("section")
    place = lax.axis_index("space")
    replicas = space // micro_count
    width = taps + channels
    layers = groups * sections
    cells = extent_x * space * extent_z
    lanes = extent_y * channels
    paired = space == 8 and replicas == 2 and sections == 4 and extent_x == 1 and extent_z == 128 and lanes == 128
    me = jnp.stack([section, place, place % replicas]).astype(jnp.int32)

    conv_rows = jnp.swapaxes(conv_weight, 2, 3)
    weights = jnp.concatenate([conv_rows[:, 0], mix_weight[:, 0]], axis=1)
    if paired:
        fields = [x.reshape(micro_count, lanes, extent_z) for x in (inputs, cotangent)]
        pieces, plan = gather_paired(weights, fields, me, place)
    else:
        both = jnp.stack([inputs, cotangent], axis=1)
        both = both.transpose(0, 1, 3, 5, 4, 2).reshape(micro_count, 2, extent_x * extent_z, lanes)
        pieces, plan = gather_plain(weights, both, place, replicas)

    total_x = extent_x * space
    act = jax.ShapeDtypeStruct((cells, lanes), F32)
    kept = [
        jax.ShapeDtypeStruct((sections, 10 * lanes, 2 * hidden), BF),
        jax.ShapeDtypeStruct((sections, cells, 2 * hidden), BF),
        jax.ShapeDtypeStruct((2, total_x + 2, extent_z, 3 * lanes), BF),
        jax.ShapeDtypeStruct((2, cells, 2 * hidden), BF),
    ]
    early = [pieces[i] for i in needed(plan, 0, 0)]
    act, folded, *state, mark = call(
        functools.partial(first_kernel, plan, len(early)),
        [act] + kept + [jax.ShapeDtypeStruct((8, 128), F32)],
        [], 2 * MIB,
        me, conv_rows, mix_weight, *early,
    )
    act, *state = call(
        functools.partial(next_kernel), [act] + kept[1:], [], 2 * MIB, me, mark, folded, into=(act, *state)
    )
    saved = (folded, *state)
    if paired:
        pieces[7] = exchange(after(pieces[5], mark), 1)
    late = [pieces[i] for i in needed(plan, 1, 1)]
    terms = jax.ShapeDtypeStruct((width // replicas, hidden), BF)
    shares = SHARES if paired else (tuple(range(28)),)
    wide = pltpu.VMEM((total_x + 2, extent_z, 9 * lanes), F32)
    whole = pltpu.VMEM((width, hidden), BF)
    grad = pltpu.VMEM((cells, 2 * hidden), BF)
    up, late_terms = call(
        functools.partial(second_kernel, shares, plan, len(late)),
        [act, terms],
        [pltpu.VMEM(x.shape, x.dtype) for x in kept] + [pltpu.VMEM((cells, lanes), F32), wide, whole, grad],
        40 * MIB,
        me, conv_rows, mix_weight, *late, act,
    )
    traded = cross(late_terms, 2, 4) if paired else None
    (early_terms,) = call(
        functools.partial(third_kernel, shares),
        [terms],
        [pltpu.VMEM((cells, lanes), F32), wide, whole, grad],
        20 * MIB,
        me, up, *saved,
    )

    factor = 1.0 / math.sqrt(micro_count * cells * extent_y)
    outs = [
        jax.ShapeDtypeStruct((groups, 1, taps, hidden), F32),
        jax.ShapeDtypeStruct((groups, 1, channels, hidden), F32),
    ]
    scratch = [pltpu.VMEM((width, hidden), F32), pltpu.SemaphoreType.DMA((2, 8))]
    grads = ()
    for group in (1, 0):
        own = late_terms if group else early_terms
        if paired:
            met = after(traded, early_terms) if group else cross(own, 2, 4)
            half = (own.astype(F32) + met.astype(F32)).astype(BF)
            other = cross(half, 4, 2)
            kernel, parts = both_kernel, (half, other, exchange(half, 1), exchange(other, 1))
        else:
            level = [own] + [exchange(own, k * replicas) for k in range(1, micro_count)]
            level = [x.astype(F32) for x in level]
            while len(level) > 1:
                level = [level[i] + level[i + 1] for i in range(0, len(level), 2)]
            rows_of = [[m * replicas + r for r in range(replicas)] for m in range(micro_count)]
            every = lax.all_gather(level[0].astype(BF), "space", axis=0, tiled=True, axis_index_groups=rows_of)
            kernel, parts = plain_kernel, (every,)
        grads = call(functools.partial(kernel, group, factor), outs, scratch, MIB // 16, me, *parts, into=grads)
    conv, mix = grads
    return (jnp.swapaxes(conv, 2, 3), mix)


def solution(mesh):
    placed = (
        P(None, None, "space", None, None),
        P(None, None, "space", None, None),
        P(None, "section", None, None),
        P(None, "section", None, None),
    )
    return jax.shard_map(
        per_device,
        mesh=mesh,
        in_specs=placed,
        out_specs=(P(None, "section", None, None), P(None, "section", None, None)),
        check_vma=False,
    )
```

```python
import functools
import math

import jax
import jax.numpy as jnp
from jax import lax
from jax.experimental import pallas as pl
from jax.experimental.pallas import tpu as pltpu
from jax.sharding import PartitionSpec as P

BF = jnp.bfloat16
F32 = jnp.float32
NT = (((1,), (1,)), ((), ()))
NN = (((1,), (0,)), ((), ()))
TN = (((0,), (0,)), ((), ()))
MIB = 1024 * 1024
SHARES = (
    (0, 3, 6, 1, 4, 7, 2, 5, 8, 9, 12, 15, 10, 13),
    (16, 11, 14, 17, 18, 21, 24, 19, 22, 25, 20, 23, 26, 27),
)


def dot(a, b, dims):
    return lax.dot_general(a, b, dims, preferred_element_type=F32)


def shifted(x, step, length):
    place = lax.broadcasted_iota(jnp.int32, x.shape, 0) % length
    edge = 0 if step > 0 else length - 1
    return jnp.where(place == edge, 0.0, pltpu.roll(x, step % x.shape[0], 0))


def fold_taps(source, start, first, count, layer, folded):
    for tap in range(first, first + count):
        row = start + 64 * (tap - first)
        block = source[row : row + 64]
        if tap == 27:
            at, places = 1152, [(0, 0), (1, 1)]
            for y, other in ((0, 1), (1, 0)):
                folded[layer, at + 64 * y : at + 64 * y + 64, 128 * other : 128 * other + 128] = jnp.zeros_like(block)
        else:
            at = 128 * (3 * (tap // 9) + tap % 3)
            places = [[(0, 1)], [(0, 0), (1, 1)], [(1, 0)]][tap // 3 % 3]
        for y, other in places:
            folded[layer, at + 64 * y : at + 64 * y + 64, 128 * other : 128 * other + 128] = block


def columns_of(padded):
    planes = padded.shape[0] - 2
    parts = [padded[d : d + planes] for d in range(3)]
    return jnp.concatenate(parts, axis=2).reshape(planes * padded.shape[1], 3 * padded.shape[2])


def forward_layer(layer, slot, act, folded, slope, keep_a, keep_h):
    padded = keep_a.at[slot]
    planes = padded.shape[0] - 2
    length = padded.shape[1]
    now = act[...]
    for at, value in enumerate((shifted(now, 1, length), now, shifted(now, -1, length))):
        padded[1 : planes + 1, :, 128 * at : 128 * at + 128] = value.astype(BF).reshape(planes, length, 128)
    pre = dot(columns_of(padded), folded[layer, :1152], NN)
    gate = 0.5 * jnp.tanh(0.5 * pre) + 0.5
    wide = pre * gate
    hidden = wide.astype(BF)
    slope[layer] = (gate + wide * (1.0 - gate)).astype(slope.dtype)
    act[...] = now + dot(hidden, folded[layer, 1152:], NT)
    keep_h[slot] = hidden


def term_rows(blocks, base, conv, mix, terms):
    for number, tap in enumerate(blocks):
        at = 128 * (3 * (tap // 9) + tap % 3 - base)
        if tap == 27:
            value = mix[:64, :128] + mix[64:, 128:]
        elif tap // 3 % 3 == 1:
            value = conv[at : at + 64, :128] + conv[at + 64 : at + 128, 128:]
        elif tap // 3 % 3 == 0:
            value = conv[at : at + 64, 128:]
        else:
            value = conv[at + 64 : at + 128, :128]
        terms[64 * number : 64 * number + 64] = value.astype(BF)


def some_columns(padded, groups):
    planes = padded.shape[0] - 2
    parts = []
    for d in range(3):
        inside = [g - 3 * d for g in groups if g // 3 == d]
        if inside:
            parts.append(padded[d : d + planes, :, 128 * inside[0] : 128 * inside[-1] + 128])
    return jnp.concatenate(parts, axis=2).reshape(planes * padded.shape[1], 128 * len(groups))


def backward_layer(shares, mine, layer, owned, up, grad, wide, folded, slope, keep_a, keep_h, terms, spread_if):
    planes = wide.shape[0] - 2
    length = wide.shape[1]
    now = up[...]
    half = now.shape[0] // 2
    for rows in (slice(0, half), slice(half, 2 * half)):
        hid_grad = dot(now[rows].astype(BF), folded[layer, 1152:], NN)
        grad[rows] = (hid_grad * slope[layer, rows]).astype(BF)

    for replica, blocks in enumerate(shares):
        groups = sorted({3 * (tap // 9) + tap % 3 for tap in blocks if tap < 27})

        @pl.when(owned & (mine == replica) if len(shares) > 1 else owned)
        def _(blocks=blocks, groups=groups):
            conv = dot(some_columns(keep_a.at[0], groups), grad[...], TN)
            mix = dot(up[...].astype(BF), keep_h[0], TN) if 27 in blocks else None
            term_rows(blocks, groups[0], conv, mix, terms)

    def spread():
        wide[1 : planes + 1] = dot(grad[...], folded[layer, :1152], NT).reshape(planes, length, 1152)
        total = up[...]
        for dz in range(3):
            part = 0.0
            for dx in range(3):
                at = 128 * (3 * dx + dz)
                part = part + wide[2 - dx : 2 - dx + planes, :, at : at + 128]
            part = part.reshape(planes * length, 128)
            total = total + (part if dz == 1 else shifted(part, dz - 1, length))
        up[...] = total

    if spread_if is None:
        spread()
    else:
        pl.when(spread_if)(spread)


def clear_edges(ref):
    ref[0] = jnp.zeros(ref.shape[1:], ref.dtype)
    ref[ref.shape[0] - 1] = jnp.zeros(ref.shape[1:], ref.dtype)


def needed(plan, group, field):
    weight_steps, plane_steps = plan(0, 0, field)
    return sorted({step[0] for step in weight_steps[group] + plane_steps})


def take(plan, me_ref, field, group, conv, mix, pieces, folded, target):
    section, place = me_ref[0], me_ref[1]
    taps = conv.shape[2] // 64
    fold_taps(conv.at[group, 0], 0, 0, taps, section, folded)
    fold_taps(mix.at[group, 0], 0, taps, 1, section, folded)
    weight_steps, plane_steps = plan(section, place, field)
    pieces = dict(zip(needed(plan, group, field), pieces, strict=True))
    for piece, start, count, layer, first, choices in weight_steps[group]:
        for choice in choices:

            @pl.when(first == choice)
            def _(piece=piece, start=start, count=count, layer=layer, choice=choice):
                fold_taps(pieces[piece], start, choice, count, layer, folded)

    for piece, start, rows, rel in plane_steps:
        row = pl.multiple_of((place ^ rel) * rows, rows)
        target[pl.ds(row, rows)] = pieces[piece][start : start + rows].astype(F32)


def begin(copies, sems, first):
    started = []
    for number, (source, target) in enumerate(copies):
        copy = pltpu.make_async_copy(source, target, sems.at[first + number])
        copy.start()
        started.append(copy)
    return started


def finish(started):
    for copy in started:
        copy.wait()


def split_kernel(me_ref, inputs, cotangent, token, own, beside, across, swap):
    chip, core = me_ref[1] // 2, me_ref[1] % 2
    old = lax.broadcasted_iota(jnp.int32, (128, 128), 0)
    new = lax.broadcasted_iota(jnp.int32, (128, 128), 1)
    order = ((old % 2) * 64 + old // 2 == new).astype(F32).astype(BF)
    for number, source in enumerate((inputs, cotangent)):
        rows = slice(128 * number, 128 * number + 128)

        def turned(offset, source=source):
            return dot(source[chip ^ offset], order, TN).astype(BF)

        mine, far = turned(0), turned(3)
        one, two = turned(1 + core), turned(2 - core)
        own[rows] = mine
        across[rows] = far
        beside[rows] = one
        swap[rows] = mine
        swap[256 + 128 * number : 384 + 128 * number] = two


def first_kernel(plan, piece_count, me_ref, conv, mix, *refs):
    pieces, refs = refs[:piece_count], refs[piece_count:]
    act, folded, slope, keep_a, keep_h, mark = refs
    section = me_ref[0]
    take(plan, me_ref, 0, 0, conv, mix, pieces, folded, act)
    for slot in range(2):
        clear_edges(keep_a.at[slot])
    mark[...] = jnp.zeros_like(mark)

    def step(layer, carry):
        forward_layer(layer, jnp.where(layer == section, 0, 1), act, folded, slope, keep_a, keep_h)
        return carry

    lax.fori_loop(0, folded.shape[0] - 1, step, 0)


def next_kernel(me_ref, mark, folded, *refs):
    act, slope, keep_a, keep_h = refs[-4:]
    layer = folded.shape[0] - 1
    forward_layer(layer, jnp.where(layer == me_ref[0], 0, 1), act, folded, slope, keep_a, keep_h)


def all_back(shares, me_ref, last, up, grad, wide, folded, slope, keep_a, keep_h, terms, out):
    section, replica = me_ref[0], me_ref[2]
    sections = folded.shape[0]
    target = out if len(shares) > 1 else terms

    def back(i, carry):
        layer = sections - 1 - i
        spread_if = None if last else layer > 0
        backward_layer(
            shares, replica, layer, layer == section, up, grad, wide, folded, slope, keep_a, keep_h, target, spread_if
        )
        return carry

    lax.fori_loop(0, sections, back, 0)
    if len(shares) == 1:
        rows = out.shape[0]
        out[...] = terms[pl.ds(pl.multiple_of(replica * rows, rows), rows)]


def second_kernel(shares, plan, piece_count, me_ref, conv, mix, *refs):
    pieces, refs = refs[:piece_count], refs[piece_count:]
    act_in, up, out, folded, slope, keep_a, keep_h, act, wide, terms, grad = refs
    section = me_ref[0]
    act[...] = act_in[...]
    take(plan, me_ref, 1, 1, conv, mix, pieces, folded, up)
    for slot in range(2):
        clear_edges(keep_a.at[slot])
    clear_edges(wide)

    def step(layer, carry):
        forward_layer(layer, jnp.where(layer == section, 0, 1), act, folded, slope, keep_a, keep_h)
        return carry

    lax.fori_loop(0, folded.shape[0], step, 0)
    all_back(shares, me_ref, True, up, grad, wide, folded, slope, keep_a, keep_h, terms, out)


def third_kernel(shares, me_ref, up_in, folded, slope, keep_a, keep_h, out, up, wide, terms, grad):
    up[...] = up_in[...]
    clear_edges(wide)
    all_back(shares, me_ref, False, up, grad, wide, folded, slope, keep_a, keep_h, terms, out)


def place_taps(taps, factor, value, whole):
    for number, tap in enumerate(taps):
        whole[64 * tap : 64 * tap + 64] = value[64 * number : 64 * number + 64] * factor


def send_whole(whole, conv, mix, group, sems):
    taps = conv.shape[2]
    copies = [(whole.at[pl.ds(row, taps // 3)], conv.at[group, 0, pl.ds(row, taps // 3)]) for row in range(0, taps, taps // 3)]
    finish(begin(copies + [(whole.at[pl.ds(taps, whole.shape[0] - taps)], mix.at[group, 0])], sems, 0))


def both_kernel(group, factor, me_ref, own_a, own_b, far_a, far_b, *refs):
    conv, mix, whole, sems = refs[-4:]
    first = me_ref[2] == 0
    own = own_a[...].astype(F32) + own_b[...].astype(F32)
    far = far_a[...].astype(F32) + far_b[...].astype(F32)
    place_taps(SHARES[0], factor, jnp.where(first, own, far), whole)
    place_taps(SHARES[1], factor, jnp.where(first, far, own), whole)
    send_whole(whole, conv, mix, group, sems)


def plain_kernel(group, factor, me_ref, terms, *refs):
    conv, mix, whole, sems = refs[-4:]
    place_taps(range(28), factor, terms[...].astype(F32), whole)
    send_whole(whole, conv, mix, group, sems)


def size_of(x):
    return math.prod(x.shape) * x.dtype.itemsize


def call(kernel, outs, scratch, traffic, *args, into=()):
    vmem = pl.BlockSpec(memory_space=pltpu.VMEM)
    far = pl.BlockSpec(memory_space=pl.ANY)
    specs = [pl.BlockSpec(memory_space=pltpu.SMEM)] + [vmem] * (len(args) - 1) + [vmem if kernel.func is next_kernel else far] * len(into)
    held = sum(size_of(x) for x in scratch if x.memory_space == pltpu.VMEM)
    passed = sum(size_of(x) for x in args) + sum(size_of(x) for x in outs)
    limit = held + held // 4 + 10 * MIB
    if held + passed > 30 * MIB:
        limit = 63 * MIB
    return pl.pallas_call(
        kernel,
        out_shape=outs,
        in_specs=specs,
        out_specs=[far if kernel.func in (both_kernel, plain_kernel) else vmem] * len(outs),
        scratch_shapes=scratch,
        input_output_aliases={len(args) + i: i for i in range(len(into))},
        compiler_params=pltpu.CompilerParams(vmem_limit_bytes=limit),
        cost_estimate=pl.CostEstimate(flops=traffic * 100, bytes_accessed=traffic, transcendentals=0),
    )(*args, *into)


def exchange(block, mask):
    count = lax.axis_size("space")
    return lax.ppermute(block, "space", [(i, i ^ mask) for i in range(count)])


def cross(block, first, second):
    count = lax.axis_size("space")
    return lax.ppermute(block, "space", [(i, i ^ (second if i % 2 else first)) for i in range(count)])


def after(x, *others):
    return lax.optimization_barrier((x, *others))[0]


def gather_paired(weights, fields, me, place):
    sections, space = lax.axis_size("section"), lax.axis_size("space")
    rows = weights.shape[1]
    half, quarter = rows // 2, rows // 4
    chip, core = place // 2, place % 2
    side = (chip // 2) ^ (chip % 2)
    mine = jnp.where(side == 0, weights[:, :half], weights[:, half:])
    part = lax.dynamic_slice_in_dim(mine, core * quarter, quarter, axis=1)
    route = []
    for s in range(sections):
        for j in range(space):
            target = (s + (-1 if j % 2 else 1)) % sections
            route.append((s * space + j, target * space + j))
    across = [(s, (s + 2) % sections) for s in range(sections)]
    token = exchange(mine[0, :16], 1)
    own, beside, diagonal, swap = call(
        functools.partial(split_kernel),
        [jax.ShapeDtypeStruct((count, 128), BF) for count in (256, 256, 256, 512)],
        [], MIB, me, *fields, token,
    )
    other = exchange(swap, 1)
    diagonal = exchange(diagonal, 6)
    near, far = [], []
    for group in range(2):
        near.append(lax.ppermute(after(mine[group], *near), ("section", "space"), route))
        far.append(lax.ppermute(after(part[group], *near[:group]), "section", across))
    sent = [beside, other[256:]]
    diagonal_far = exchange(diagonal, 1)
    here = [jnp.concatenate([near[g], far[g]] + (sent if g == 0 else []), axis=0) for g in range(2)]
    here[0] = after(here[0], diagonal)
    there = [cross(x, 2, 4) for x in here]
    late = exchange(here[1], 1)
    ready = after(there[0], late)
    pieces = [here[0], there[0], exchange(here[0], 1), exchange(ready[:half], 1), here[1], there[1], late, None]
    planes = [own, other, diagonal, diagonal_far, exchange(ready[half:], 1)]
    plane_rows = 128

    def plan(section, place, field):
        chip, core = place // 2, place % 2
        side = (chip // 2) ^ (chip % 2)

        def where(piece, row):
            return (12, row - half) if piece == 3 and row >= half else (piece, row)

        weight_steps = []
        for group in range(2):
            steps = []
            for swapped in range(2):
                source = core ^ swapped
                beside = lax.rem(section + sections - 1 + 2 * source, sections)
                across = lax.rem(section + 2, sections)
                for other in range(2):
                    piece = 4 * group + 2 * swapped + other
                    first = (side ^ other) * 14
                    steps.append((piece, 0, 14, beside, first, (0, 14)))
                    steps.append((*where(piece, half), 7, across, first + source * 7, (0, 7, 14, 21)))
            weight_steps.append(steps)
        plane_steps = []
        start = field * plane_rows
        for piece, rel in ((8, 0), (9, 1), (10, 6), (11, 7)):
            plane_steps.append((piece, start, plane_rows, rel))
        for swapped in range(2):
            rel = swapped ^ (2 + 2 * (core ^ swapped))
            start = half + quarter + field * plane_rows
            plane_steps.append((*where(1 + 2 * swapped, start), plane_rows, rel))
            plane_steps.append((*where(1 + 2 * swapped, start + 2 * plane_rows), plane_rows, rel ^ 1))
        return weight_steps, plane_steps

    return pieces + planes, plan


def gather_plain(weights, both, place, replicas):
    sections = lax.axis_size("section")
    micro_count, _, plane_rows, _ = both.shape
    routes = [[(i, (i + d) % sections) for i in range(sections)] for d in range(1, sections)]
    pieces = [lax.ppermute(group, "section", route) for group in weights for route in routes]
    near = []
    for k in range(micro_count):
        part = lax.dynamic_index_in_dim(both, (place // replicas) ^ k, 0, keepdims=False)
        near.append(part if k == 0 else exchange(part, k * replicas))
    near = jnp.stack(near)
    fields = [near] + [exchange(near, r) for r in range(1, replicas)]
    fields = [x.reshape(-1, x.shape[-1]) for x in fields]

    def plan(section, place, field):
        first = weights.shape[0] * (sections - 1)
        weight_steps = [
            [
                (group * (sections - 1) + d - 1, 0, weights.shape[1] // 64, lax.rem(section + sections - d, sections), 0, (0,))
                for d in range(1, sections)
            ]
            for group in range(weights.shape[0])
        ]
        plane_steps = [
            (first + r, (2 * k + field) * plane_rows, plane_rows, k * replicas + r)
            for k in range(micro_count)
            for r in range(replicas)
        ]
        return weight_steps, plane_steps

    return pieces + fields, plan


def per_device(inputs, cotangent, conv_weight, mix_weight):
    micro_count, channels, extent_x, extent_y, extent_z = inputs.shape
    groups, _, hidden, taps = conv_weight.shape
    sections = lax.axis_size("section")
    space = lax.axis_size("space")
    section = lax.axis_index("section")
    place = lax.axis_index("space")
    replicas = space // micro_count
    width = taps + channels
    layers = groups * sections
    cells = extent_x * space * extent_z
    lanes = extent_y * channels
    paired = space == 8 and replicas == 2 and sections == 4 and extent_x == 1 and extent_z == 128 and lanes == 128
    me = jnp.stack([section, place, place % replicas]).astype(jnp.int32)

    conv_rows = jnp.swapaxes(conv_weight, 2, 3)
    weights = jnp.concatenate([conv_rows[:, 0], mix_weight[:, 0]], axis=1)
    if paired:
        fields = [x.reshape(micro_count, lanes, extent_z) for x in (inputs, cotangent)]
        pieces, plan = gather_paired(weights, fields, me, place)
    else:
        both = jnp.stack([inputs, cotangent], axis=1)
        both = both.transpose(0, 1, 3, 5, 4, 2).reshape(micro_count, 2, extent_x * extent_z, lanes)
        pieces, plan = gather_plain(weights, both, place, replicas)

    total_x = extent_x * space
    act = jax.ShapeDtypeStruct((cells, lanes), F32)
    kept = [
        jax.ShapeDtypeStruct((sections, 10 * lanes, 2 * hidden), BF),
        jax.ShapeDtypeStruct((sections, cells, 2 * hidden), BF),
        jax.ShapeDtypeStruct((2, total_x + 2, extent_z, 3 * lanes), BF),
        jax.ShapeDtypeStruct((2, cells, 2 * hidden), BF),
    ]
    early = [pieces[i] for i in needed(plan, 0, 0)]
    act, folded, *state, mark = call(
        functools.partial(first_kernel, plan, len(early)),
        [act] + kept + [jax.ShapeDtypeStruct((8, 128), F32)],
        [], 2 * MIB,
        me, conv_rows, mix_weight, *early,
    )
    act, *state = call(
        functools.partial(next_kernel), [act] + kept[1:], [], 2 * MIB, me, mark, folded, into=(act, *state)
    )
    saved = (folded, *state)
    if paired:
        pieces[7] = exchange(after(pieces[5], mark), 1)
    late = [pieces[i] for i in needed(plan, 1, 1)]
    terms = jax.ShapeDtypeStruct((width // replicas, hidden), BF)
    shares = SHARES if paired else (tuple(range(28)),)
    wide = pltpu.VMEM((total_x + 2, extent_z, 9 * lanes), F32)
    whole = pltpu.VMEM((width, hidden), BF)
    grad = pltpu.VMEM((cells, 2 * hidden), BF)
    up, late_terms = call(
        functools.partial(second_kernel, shares, plan, len(late)),
        [act, terms],
        [pltpu.VMEM(x.shape, x.dtype) for x in kept] + [pltpu.VMEM((cells, lanes), F32), wide, whole, grad],
        40 * MIB,
        me, conv_rows, mix_weight, *late, act,
    )
    traded = cross(late_terms, 2, 4) if paired else None
    (early_terms,) = call(
        functools.partial(third_kernel, shares),
        [terms],
        [pltpu.VMEM((cells, lanes), F32), wide, whole, grad],
        20 * MIB,
        me, up, *saved,
    )

    factor = 1.0 / math.sqrt(micro_count * cells * extent_y)
    outs = [
        jax.ShapeDtypeStruct((groups, 1, taps, hidden), F32),
        jax.ShapeDtypeStruct((groups, 1, channels, hidden), F32),
    ]
    scratch = [pltpu.VMEM((width, hidden), F32), pltpu.SemaphoreType.DMA((4,))]
    grads = ()
    for group in (1, 0):
        own = late_terms if group else early_terms
        if paired:
            met = after(traded, early_terms) if group else cross(own, 2, 4)
            half = (own.astype(F32) + met.astype(F32)).astype(BF)
            other = cross(half, 4, 2)
            kernel, parts = both_kernel, (half, other, exchange(half, 1), exchange(other, 1))
        else:
            level = [own] + [exchange(own, k * replicas) for k in range(1, micro_count)]
            level = [x.astype(F32) for x in level]
            while len(level) > 1:
                level = [level[i] + level[i + 1] for i in range(0, len(level), 2)]
            rows_of = [[m * replicas + r for r in range(replicas)] for m in range(micro_count)]
            every = lax.all_gather(level[0].astype(BF), "space", axis=0, tiled=True, axis_index_groups=rows_of)
            kernel, parts = plain_kernel, (every,)
        grads = call(functools.partial(kernel, group, factor), outs, scratch, MIB // 16, me, *parts, into=grads)
    conv, mix = grads
    return (jnp.swapaxes(conv, 2, 3), mix)


def solution(mesh):
    placed = (
        P(None, None, "space", None, None),
        P(None, None, "space", None, None),
        P(None, "section", None, None),
        P(None, "section", None, None),
    )
    return jax.shard_map(
        per_device,
        mesh=mesh,
        in_specs=placed,
        out_specs=(P(None, "section", None, None), P(None, "section", None, None)),
        check_vma=False,
    )
```

```python
import functools
import math

import jax
import jax.numpy as jnp
from jax import lax
from jax.experimental import pallas as pl
from jax.experimental.pallas import tpu as pltpu
from jax.sharding import PartitionSpec as P

BF = jnp.bfloat16
F32 = jnp.float32
NT = (((1,), (1,)), ((), ()))
NN = (((1,), (0,)), ((), ()))
TN = (((0,), (0,)), ((), ()))
MIB = 1024 * 1024
SHARES = (
    (0, 3, 6, 1, 4, 7, 2, 5, 8, 9, 12, 15, 10, 13),
    (16, 11, 14, 17, 18, 21, 24, 19, 22, 25, 20, 23, 26, 27),
)


def dot(a, b, dims):
    return lax.dot_general(a, b, dims, preferred_element_type=F32)


def shifted(x, step, length):
    place = lax.broadcasted_iota(jnp.int32, x.shape, 0) % length
    edge = 0 if step > 0 else length - 1
    return jnp.where(place == edge, 0.0, pltpu.roll(x, step % x.shape[0], 0))


def fold_taps(source, start, first, count, layer, folded):
    for tap in range(first, first + count):
        row = start + 64 * (tap - first)
        block = source[row : row + 64]
        if tap == 27:
            at, places = 1152, [(0, 0), (1, 1)]
            for y, other in ((0, 1), (1, 0)):
                folded[layer, at + 64 * y : at + 64 * y + 64, 128 * other : 128 * other + 128] = jnp.zeros_like(block)
        else:
            at = 128 * (3 * (tap // 9) + tap % 3)
            places = [[(0, 1)], [(0, 0), (1, 1)], [(1, 0)]][tap // 3 % 3]
        for y, other in places:
            folded[layer, at + 64 * y : at + 64 * y + 64, 128 * other : 128 * other + 128] = block


def columns_of(padded):
    planes = padded.shape[0] - 2
    parts = [padded[d : d + planes] for d in range(3)]
    return jnp.concatenate(parts, axis=2).reshape(planes * padded.shape[1], 3 * padded.shape[2])


def forward_layer(layer, slot, act, folded, slope, keep_a, keep_h, mix_if=None):
    padded = keep_a.at[slot]
    planes = padded.shape[0] - 2
    length = padded.shape[1]
    now = act[...]
    for at, value in enumerate((shifted(now, 1, length), now, shifted(now, -1, length))):
        padded[1 : planes + 1, :, 128 * at : 128 * at + 128] = value.astype(BF).reshape(planes, length, 128)
    pre = dot(columns_of(padded), folded[layer, :1152], NN)
    gate = 0.5 * jnp.tanh(0.5 * pre) + 0.5
    wide = pre * gate
    hidden = wide.astype(BF)
    slope[layer] = (gate + wide * (1.0 - gate)).astype(slope.dtype)
    keep_h[slot] = hidden

    def mix():
        act[...] = now + dot(hidden, folded[layer, 1152:], NT)

    if mix_if is None:
        mix()
    else:
        pl.when(mix_if)(mix)


def term_rows(blocks, base, conv, mix, terms):
    for number, tap in enumerate(blocks):
        at = 128 * (3 * (tap // 9) + tap % 3 - base)
        if tap == 27:
            value = mix[:64, :128] + mix[64:, 128:]
        elif tap // 3 % 3 == 1:
            value = conv[at : at + 64, :128] + conv[at + 64 : at + 128, 128:]
        elif tap // 3 % 3 == 0:
            value = conv[at : at + 64, 128:]
        else:
            value = conv[at + 64 : at + 128, :128]
        terms[64 * number : 64 * number + 64] = value.astype(BF)


def some_columns(padded, groups):
    planes = padded.shape[0] - 2
    parts = []
    for d in range(3):
        inside = [g - 3 * d for g in groups if g // 3 == d]
        if inside:
            parts.append(padded[d : d + planes, :, 128 * inside[0] : 128 * inside[-1] + 128])
    return jnp.concatenate(parts, axis=2).reshape(planes * padded.shape[1], 128 * len(groups))


def backward_layer(shares, mine, layer, owned, up, grad, wide, folded, slope, keep_a, keep_h, terms, spread_if):
    planes = wide.shape[0] - 2
    length = wide.shape[1]
    now = up[...]
    half = now.shape[0] // 2
    for rows in (slice(0, half), slice(half, 2 * half)):
        hid_grad = dot(now[rows].astype(BF), folded[layer, 1152:], NN)
        grad[rows] = (hid_grad * slope[layer, rows]).astype(BF)

    for replica, blocks in enumerate(shares):
        groups = sorted({3 * (tap // 9) + tap % 3 for tap in blocks if tap < 27})

        @pl.when(owned & (mine == replica) if len(shares) > 1 else owned)
        def _(blocks=blocks, groups=groups):
            conv = dot(some_columns(keep_a.at[0], groups), grad[...], TN)
            mix = dot(up[...].astype(BF), keep_h[0], TN) if 27 in blocks else None
            term_rows(blocks, groups[0], conv, mix, terms)

    def spread():
        wide[1 : planes + 1] = dot(grad[...], folded[layer, :1152], NT).reshape(planes, length, 1152)
        total = up[...]
        for dz in range(3):
            part = 0.0
            for dx in range(3):
                at = 128 * (3 * dx + dz)
                part = part + wide[2 - dx : 2 - dx + planes, :, at : at + 128]
            part = part.reshape(planes * length, 128)
            total = total + (part if dz == 1 else shifted(part, dz - 1, length))
        up[...] = total

    if spread_if is None:
        spread()
    else:
        pl.when(spread_if)(spread)


def clear_edges(ref):
    ref[0] = jnp.zeros(ref.shape[1:], ref.dtype)
    ref[ref.shape[0] - 1] = jnp.zeros(ref.shape[1:], ref.dtype)


def needed(plan, group, field):
    weight_steps, plane_steps = plan(0, 0, field)
    return sorted({step[0] for step in weight_steps[group] + plane_steps})


def take(plan, me_ref, field, group, conv, mix, pieces, folded, target):
    section, place = me_ref[0], me_ref[1]
    taps = conv.shape[2] // 64
    fold_taps(conv.at[group, 0], 0, 0, taps, section, folded)
    fold_taps(mix.at[group, 0], 0, taps, 1, section, folded)
    weight_steps, plane_steps = plan(section, place, field)
    pieces = dict(zip(needed(plan, group, field), pieces, strict=True))
    for piece, start, count, layer, first, choices in weight_steps[group]:
        for choice in choices:

            @pl.when(first == choice)
            def _(piece=piece, start=start, count=count, layer=layer, choice=choice):
                fold_taps(pieces[piece], start, choice, count, layer, folded)

    for piece, start, rows, rel in plane_steps:
        row = pl.multiple_of((place ^ rel) * rows, rows)
        target[pl.ds(row, rows)] = pieces[piece][start : start + rows].astype(F32)


def begin(copies, sems, first):
    started = []
    for number, (source, target) in enumerate(copies):
        copy = pltpu.make_async_copy(source, target, sems.at[first + number])
        copy.start()
        started.append(copy)
    return started


def finish(started):
    for copy in started:
        copy.wait()


def split_kernel(me_ref, inputs, cotangent, token, own, beside, across, swap):
    chip, core = me_ref[1] // 2, me_ref[1] % 2
    old = lax.broadcasted_iota(jnp.int32, (128, 128), 0)
    new = lax.broadcasted_iota(jnp.int32, (128, 128), 1)
    order = ((old % 2) * 64 + old // 2 == new).astype(F32).astype(BF)
    for number, source in enumerate((inputs, cotangent)):
        rows = slice(128 * number, 128 * number + 128)

        def turned(offset, source=source):
            return dot(source[chip ^ offset], order, TN).astype(BF)

        mine, far = turned(0), turned(3)
        one, two = turned(1 + core), turned(2 - core)
        own[rows] = mine
        across[rows] = far
        beside[rows] = one
        swap[rows] = mine
        swap[256 + 128 * number : 384 + 128 * number] = two


def first_kernel(plan, piece_count, me_ref, conv, mix, *refs):
    pieces, refs = refs[:piece_count], refs[piece_count:]
    act, folded, slope, keep_a, keep_h, mark = refs
    section = me_ref[0]
    take(plan, me_ref, 0, 0, conv, mix, pieces, folded, act)
    for slot in range(2):
        clear_edges(keep_a.at[slot])
    mark[...] = jnp.zeros_like(mark)

    def step(layer, carry):
        forward_layer(layer, jnp.where(layer == section, 0, 1), act, folded, slope, keep_a, keep_h)
        return carry

    lax.fori_loop(0, folded.shape[0] - 1, step, 0)


def next_kernel(me_ref, mark, folded, *refs):
    act, slope, keep_a, keep_h = refs[-4:]
    layer = folded.shape[0] - 1
    forward_layer(layer, jnp.where(layer == me_ref[0], 0, 1), act, folded, slope, keep_a, keep_h)


def all_back(shares, me_ref, last, up, grad, wide, folded, slope, keep_a, keep_h, terms, out):
    section, replica = me_ref[0], me_ref[2]
    sections = folded.shape[0]
    target = out if len(shares) > 1 else terms

    def back(i, carry):
        layer = sections - 1 - i
        spread_if = None if last else layer > 0
        backward_layer(
            shares, replica, layer, layer == section, up, grad, wide, folded, slope, keep_a, keep_h, target, spread_if
        )
        return carry

    lax.fori_loop(0, sections, back, 0)
    if len(shares) == 1:
        rows = out.shape[0]
        out[...] = terms[pl.ds(pl.multiple_of(replica * rows, rows), rows)]


def second_kernel(shares, plan, piece_count, me_ref, conv, mix, *refs):
    pieces, refs = refs[:piece_count], refs[piece_count:]
    act_in, up, out, folded, slope, keep_a, keep_h, act, wide, terms, grad = refs
    section = me_ref[0]
    act[...] = act_in[...]
    take(plan, me_ref, 1, 1, conv, mix, pieces, folded, up)
    for slot in range(2):
        clear_edges(keep_a.at[slot])
    clear_edges(wide)

    def step(layer, carry):
        forward_layer(layer, jnp.where(layer == section, 0, 1), act, folded, slope, keep_a, keep_h, layer < folded.shape[0] - 1)
        return carry

    lax.fori_loop(0, folded.shape[0], step, 0)
    all_back(shares, me_ref, True, up, grad, wide, folded, slope, keep_a, keep_h, terms, out)


def third_kernel(shares, me_ref, up_in, folded, slope, keep_a, keep_h, out, up, wide, terms, grad):
    up[...] = up_in[...]
    clear_edges(wide)
    all_back(shares, me_ref, False, up, grad, wide, folded, slope, keep_a, keep_h, terms, out)


def place_taps(taps, factor, value, whole):
    for number, tap in enumerate(taps):
        whole[64 * tap : 64 * tap + 64] = value[64 * number : 64 * number + 64] * factor


def send_whole(whole, conv, mix, group, sems):
    taps = conv.shape[2]
    copies = [(whole.at[pl.ds(row, taps // 3)], conv.at[group, 0, pl.ds(row, taps // 3)]) for row in range(0, taps, taps // 3)]
    finish(begin(copies + [(whole.at[pl.ds(taps, whole.shape[0] - taps)], mix.at[group, 0])], sems, 0))


def both_kernel(group, factor, me_ref, own_a, own_b, far_a, far_b, *refs):
    conv, mix, whole, sems = refs[-4:]
    first = me_ref[2] == 0
    own = own_a[...].astype(F32) + own_b[...].astype(F32)
    far = far_a[...].astype(F32) + far_b[...].astype(F32)
    place_taps(SHARES[0], factor, jnp.where(first, own, far), whole)
    place_taps(SHARES[1], factor, jnp.where(first, far, own), whole)
    send_whole(whole, conv, mix, group, sems)


def plain_kernel(group, factor, me_ref, terms, *refs):
    conv, mix, whole, sems = refs[-4:]
    place_taps(range(28), factor, terms[...].astype(F32), whole)
    send_whole(whole, conv, mix, group, sems)


def size_of(x):
    return math.prod(x.shape) * x.dtype.itemsize


def call(kernel, outs, scratch, traffic, *args, into=()):
    vmem = pl.BlockSpec(memory_space=pltpu.VMEM)
    far = pl.BlockSpec(memory_space=pl.ANY)
    specs = [pl.BlockSpec(memory_space=pltpu.SMEM)] + [vmem] * (len(args) - 1) + [vmem if kernel.func is next_kernel else far] * len(into)
    held = sum(size_of(x) for x in scratch if x.memory_space == pltpu.VMEM)
    passed = sum(size_of(x) for x in args) + sum(size_of(x) for x in outs)
    limit = held + held // 4 + 10 * MIB
    if held + passed > 30 * MIB:
        limit = 63 * MIB
    return pl.pallas_call(
        kernel,
        out_shape=outs,
        in_specs=specs,
        out_specs=[far if kernel.func in (both_kernel, plain_kernel) else vmem] * len(outs),
        scratch_shapes=scratch,
        input_output_aliases={len(args) + i: i for i in range(len(into))},
        compiler_params=pltpu.CompilerParams(vmem_limit_bytes=limit),
        cost_estimate=pl.CostEstimate(flops=traffic * 100, bytes_accessed=traffic, transcendentals=0),
    )(*args, *into)


def exchange(block, mask):
    count = lax.axis_size("space")
    return lax.ppermute(block, "space", [(i, i ^ mask) for i in range(count)])


def cross(block, first, second):
    count = lax.axis_size("space")
    return lax.ppermute(block, "space", [(i, i ^ (second if i % 2 else first)) for i in range(count)])


def after(x, *others):
    return lax.optimization_barrier((x, *others))[0]


def gather_paired(weights, fields, me, place):
    sections, space = lax.axis_size("section"), lax.axis_size("space")
    rows = weights.shape[1]
    half, quarter = rows // 2, rows // 4
    chip, core = place // 2, place % 2
    side = (chip // 2) ^ (chip % 2)
    mine = jnp.where(side == 0, weights[:, :half], weights[:, half:])
    part = lax.dynamic_slice_in_dim(mine, core * quarter, quarter, axis=1)
    route = []
    for s in range(sections):
        for j in range(space):
            target = (s + (-1 if j % 2 else 1)) % sections
            route.append((s * space + j, target * space + j))
    across = [(s, (s + 2) % sections) for s in range(sections)]
    token = exchange(mine[0, :16], 1)
    own, beside, diagonal, swap = call(
        functools.partial(split_kernel),
        [jax.ShapeDtypeStruct((count, 128), BF) for count in (256, 256, 256, 512)],
        [], MIB, me, *fields, token,
    )
    other = exchange(swap, 1)
    diagonal = exchange(diagonal, 6)
    near, far = [], []
    for group in range(2):
        near.append(lax.ppermute(after(mine[group], *near), ("section", "space"), route))
        far.append(lax.ppermute(after(part[group], *near[:group]), "section", across))
    sent = [beside, other[256:]]
    diagonal_far = exchange(diagonal, 1)
    here = [jnp.concatenate([near[g], far[g]] + (sent if g == 0 else []), axis=0) for g in range(2)]
    here[0] = after(here[0], diagonal)
    there = [cross(x, 2, 4) for x in here]
    late = exchange(here[1], 1)
    ready = after(there[0], late)
    pieces = [here[0], there[0], exchange(here[0], 1), exchange(ready[:half], 1), here[1], there[1], late, None]
    planes = [own, other, diagonal, diagonal_far, exchange(ready[half:], 1)]
    plane_rows = 128

    def plan(section, place, field):
        chip, core = place // 2, place % 2
        side = (chip // 2) ^ (chip % 2)

        def where(piece, row):
            return (12, row - half) if piece == 3 and row >= half else (piece, row)

        weight_steps = []
        for group in range(2):
            steps = []
            for swapped in range(2):
                source = core ^ swapped
                beside = lax.rem(section + sections - 1 + 2 * source, sections)
                across = lax.rem(section + 2, sections)
                for other in range(2):
                    piece = 4 * group + 2 * swapped + other
                    first = (side ^ other) * 14
                    steps.append((piece, 0, 14, beside, first, (0, 14)))
                    steps.append((*where(piece, half), 7, across, first + source * 7, (0, 7, 14, 21)))
            weight_steps.append(steps)
        plane_steps = []
        start = field * plane_rows
        for piece, rel in ((8, 0), (9, 1), (10, 6), (11, 7)):
            plane_steps.append((piece, start, plane_rows, rel))
        for swapped in range(2):
            rel = swapped ^ (2 + 2 * (core ^ swapped))
            start = half + quarter + field * plane_rows
            plane_steps.append((*where(1 + 2 * swapped, start), plane_rows, rel))
            plane_steps.append((*where(1 + 2 * swapped, start + 2 * plane_rows), plane_rows, rel ^ 1))
        return weight_steps, plane_steps

    return pieces + planes, plan


def gather_plain(weights, both, place, replicas):
    sections = lax.axis_size("section")
    micro_count, _, plane_rows, _ = both.shape
    routes = [[(i, (i + d) % sections) for i in range(sections)] for d in range(1, sections)]
    pieces = [lax.ppermute(group, "section", route) for group in weights for route in routes]
    near = []
    for k in range(micro_count):
        part = lax.dynamic_index_in_dim(both, (place // replicas) ^ k, 0, keepdims=False)
        near.append(part if k == 0 else exchange(part, k * replicas))
    near = jnp.stack(near)
    fields = [near] + [exchange(near, r) for r in range(1, replicas)]
    fields = [x.reshape(-1, x.shape[-1]) for x in fields]

    def plan(section, place, field):
        first = weights.shape[0] * (sections - 1)
        weight_steps = [
            [
                (group * (sections - 1) + d - 1, 0, weights.shape[1] // 64, lax.rem(section + sections - d, sections), 0, (0,))
                for d in range(1, sections)
            ]
            for group in range(weights.shape[0])
        ]
        plane_steps = [
            (first + r, (2 * k + field) * plane_rows, plane_rows, k * replicas + r)
            for k in range(micro_count)
            for r in range(replicas)
        ]
        return weight_steps, plane_steps

    return pieces + fields, plan


def per_device(inputs, cotangent, conv_weight, mix_weight):
    micro_count, channels, extent_x, extent_y, extent_z = inputs.shape
    groups, _, hidden, taps = conv_weight.shape
    sections = lax.axis_size("section")
    space = lax.axis_size("space")
    section = lax.axis_index("section")
    place = lax.axis_index("space")
    replicas = space // micro_count
    width = taps + channels
    layers = groups * sections
    cells = extent_x * space * extent_z
    lanes = extent_y * channels
    paired = space == 8 and replicas == 2 and sections == 4 and extent_x == 1 and extent_z == 128 and lanes == 128
    me = jnp.stack([section, place, place % replicas]).astype(jnp.int32)

    conv_rows = jnp.swapaxes(conv_weight, 2, 3)
    weights = jnp.concatenate([conv_rows[:, 0], mix_weight[:, 0]], axis=1)
    if paired:
        fields = [x.reshape(micro_count, lanes, extent_z) for x in (inputs, cotangent)]
        pieces, plan = gather_paired(weights, fields, me, place)
    else:
        both = jnp.stack([inputs, cotangent], axis=1)
        both = both.transpose(0, 1, 3, 5, 4, 2).reshape(micro_count, 2, extent_x * extent_z, lanes)
        pieces, plan = gather_plain(weights, both, place, replicas)

    total_x = extent_x * space
    act = jax.ShapeDtypeStruct((cells, lanes), F32)
    kept = [
        jax.ShapeDtypeStruct((sections, 10 * lanes, 2 * hidden), BF),
        jax.ShapeDtypeStruct((sections, cells, 2 * hidden), BF),
        jax.ShapeDtypeStruct((2, total_x + 2, extent_z, 3 * lanes), BF),
        jax.ShapeDtypeStruct((2, cells, 2 * hidden), BF),
    ]
    early = [pieces[i] for i in needed(plan, 0, 0)]
    act, folded, *state, mark = call(
        functools.partial(first_kernel, plan, len(early)),
        [act] + kept + [jax.ShapeDtypeStruct((8, 128), F32)],
        [], 2 * MIB,
        me, conv_rows, mix_weight, *early,
    )
    act, *state = call(
        functools.partial(next_kernel), [act] + kept[1:], [], 2 * MIB, me, mark, folded, into=(act, *state)
    )
    saved = (folded, *state)
    if paired:
        pieces[7] = exchange(after(pieces[5], mark), 1)
    late = [pieces[i] for i in needed(plan, 1, 1)]
    terms = jax.ShapeDtypeStruct((width // replicas, hidden), BF)
    shares = SHARES if paired else (tuple(range(28)),)
    wide = pltpu.VMEM((total_x + 2, extent_z, 9 * lanes), F32)
    whole = pltpu.VMEM((width, hidden), BF)
    grad = pltpu.VMEM((cells, 2 * hidden), BF)
    up, late_terms = call(
        functools.partial(second_kernel, shares, plan, len(late)),
        [act, terms],
        [pltpu.VMEM(x.shape, x.dtype) for x in kept] + [pltpu.VMEM((cells, lanes), F32), wide, whole, grad],
        40 * MIB,
        me, conv_rows, mix_weight, *late, act,
    )
    traded = cross(late_terms, 2, 4) if paired else None
    (early_terms,) = call(
        functools.partial(third_kernel, shares),
        [terms],
        [pltpu.VMEM((cells, lanes), F32), wide, whole, grad],
        20 * MIB,
        me, up, *saved,
    )

    factor = 1.0 / math.sqrt(micro_count * cells * extent_y)
    outs = [
        jax.ShapeDtypeStruct((groups, 1, taps, hidden), F32),
        jax.ShapeDtypeStruct((groups, 1, channels, hidden), F32),
    ]
    scratch = [pltpu.VMEM((width, hidden), F32), pltpu.SemaphoreType.DMA((4,))]
    grads = ()
    for group in (1, 0):
        own = late_terms if group else early_terms
        if paired:
            met = after(traded, early_terms) if group else cross(own, 2, 4)
            half = (own.astype(F32) + met.astype(F32)).astype(BF)
            other = cross(half, 4, 2)
            kernel, parts = both_kernel, (half, other, exchange(half, 1), exchange(other, 1))
        else:
            level = [own] + [exchange(own, k * replicas) for k in range(1, micro_count)]
            level = [x.astype(F32) for x in level]
            while len(level) > 1:
                level = [level[i] + level[i + 1] for i in range(0, len(level), 2)]
            rows_of = [[m * replicas + r for r in range(replicas)] for m in range(micro_count)]
            every = lax.all_gather(level[0].astype(BF), "space", axis=0, tiled=True, axis_index_groups=rows_of)
            kernel, parts = plain_kernel, (every,)
        grads = call(functools.partial(kernel, group, factor), outs, scratch, MIB // 16, me, *parts, into=grads)
    conv, mix = grads
    return (jnp.swapaxes(conv, 2, 3), mix)


def solution(mesh):
    placed = (
        P(None, None, "space", None, None),
        P(None, None, "space", None, None),
        P(None, "section", None, None),
        P(None, "section", None, None),
    )
    return jax.shard_map(
        per_device,
        mesh=mesh,
        in_specs=placed,
        out_specs=(P(None, "section", None, None), P(None, "section", None, None)),
        check_vma=False,
    )
```

```python
import functools
import math

import jax
import jax.numpy as jnp
from jax import lax
from jax.experimental import pallas as pl
from jax.experimental.pallas import tpu as pltpu
from jax.sharding import PartitionSpec as P

BF = jnp.bfloat16
F32 = jnp.float32
NT = (((1,), (1,)), ((), ()))
NN = (((1,), (0,)), ((), ()))
TN = (((0,), (0,)), ((), ()))
MIB = 1024 * 1024
SHARES = (
    (0, 3, 6, 1, 4, 7, 2, 5, 8, 9, 12, 15, 10, 13),
    (16, 11, 14, 17, 18, 21, 24, 19, 22, 25, 20, 23, 26, 27),
)


def dot(a, b, dims):
    return lax.dot_general(a, b, dims, preferred_element_type=F32)


def shifted(x, step, length):
    place = lax.broadcasted_iota(jnp.int32, x.shape, 0) % length
    edge = 0 if step > 0 else length - 1
    return jnp.where(place == edge, 0.0, pltpu.roll(x, step % x.shape[0], 0))


def fold_taps(source, start, first, count, layer, folded):
    for tap in range(first, first + count):
        row = start + 64 * (tap - first)
        block = source[row : row + 64]
        if tap == 27:
            at, places = 1152, [(0, 0), (1, 1)]
            for y, other in ((0, 1), (1, 0)):
                folded[layer, at + 64 * y : at + 64 * y + 64, 128 * other : 128 * other + 128] = jnp.zeros_like(block)
        else:
            at = 128 * (3 * (tap // 9) + tap % 3)
            places = [[(0, 1)], [(0, 0), (1, 1)], [(1, 0)]][tap // 3 % 3]
        for y, other in places:
            folded[layer, at + 64 * y : at + 64 * y + 64, 128 * other : 128 * other + 128] = block


def columns_of(padded):
    planes = padded.shape[0] - 2
    parts = [padded[d : d + planes] for d in range(3)]
    return jnp.concatenate(parts, axis=2).reshape(planes * padded.shape[1], 3 * padded.shape[2])


def forward_layer(layer, slot, act, folded, slope, keep_a, keep_h, mix_if=None):
    padded = keep_a.at[slot]
    planes = padded.shape[0] - 2
    length = padded.shape[1]
    now = act[...]
    for at, value in enumerate((shifted(now, 1, length), now, shifted(now, -1, length))):
        padded[1 : planes + 1, :, 128 * at : 128 * at + 128] = value.astype(BF).reshape(planes, length, 128)
    pre = dot(columns_of(padded), folded[layer, :1152], NN)
    gate = 0.5 * jnp.tanh(0.5 * pre) + 0.5
    wide = pre * gate
    hidden = wide.astype(BF)
    slope[layer] = (gate + wide * (1.0 - gate)).astype(slope.dtype)
    keep_h[slot] = hidden

    def mix():
        act[...] = now + dot(hidden, folded[layer, 1152:], NT)

    if mix_if is None:
        mix()
    else:
        pl.when(mix_if)(mix)


def term_rows(blocks, base, conv, mix, terms):
    for number, tap in enumerate(blocks):
        at = 128 * (3 * (tap // 9) + tap % 3 - base)
        if tap == 27:
            value = mix[:64, :128] + mix[64:, 128:]
        elif tap // 3 % 3 == 1:
            value = conv[at : at + 64, :128] + conv[at + 64 : at + 128, 128:]
        elif tap // 3 % 3 == 0:
            value = conv[at : at + 64, 128:]
        else:
            value = conv[at + 64 : at + 128, :128]
        terms[64 * number : 64 * number + 64] = value.astype(BF)


def some_columns(padded, groups):
    planes = padded.shape[0] - 2
    parts = []
    for d in range(3):
        inside = [g - 3 * d for g in groups if g // 3 == d]
        if inside:
            parts.append(padded[d : d + planes, :, 128 * inside[0] : 128 * inside[-1] + 128])
    return jnp.concatenate(parts, axis=2).reshape(planes * padded.shape[1], 128 * len(groups))


def backward_layer(shares, mine, layer, owned, up, grad, wide, folded, slope, keep_a, keep_h, terms, spread_if):
    planes = wide.shape[0] - 2
    length = wide.shape[1]
    now = up[...]
    half = now.shape[0] // 2
    for rows in (slice(0, half), slice(half, 2 * half)):
        hid_grad = dot(now[rows].astype(BF), folded[layer, 1152:], NN)
        grad[rows] = (hid_grad * slope[layer, rows]).astype(BF)

    for replica, blocks in enumerate(shares):
        groups = sorted({3 * (tap // 9) + tap % 3 for tap in blocks if tap < 27})

        @pl.when(owned & (mine == replica) if len(shares) > 1 else owned)
        def _(blocks=blocks, groups=groups):
            conv = dot(some_columns(keep_a.at[0], groups), grad[...], TN)
            mix = dot(up[...].astype(BF), keep_h[0], TN) if 27 in blocks else None
            term_rows(blocks, groups[0], conv, mix, terms)

    def spread():
        wide[1 : planes + 1] = dot(grad[...], folded[layer, :1152], NT).reshape(planes, length, 1152)
        total = up[...]
        for dz in range(3):
            part = 0.0
            for dx in range(3):
                at = 128 * (3 * dx + dz)
                part = part + wide[2 - dx : 2 - dx + planes, :, at : at + 128]
            part = part.reshape(planes * length, 128)
            total = total + (part if dz == 1 else shifted(part, dz - 1, length))
        up[...] = total

    if spread_if is None:
        spread()
    else:
        pl.when(spread_if)(spread)


def clear_edges(ref):
    ref[0] = jnp.zeros(ref.shape[1:], ref.dtype)
    ref[ref.shape[0] - 1] = jnp.zeros(ref.shape[1:], ref.dtype)


def needed(plan, group, field):
    weight_steps, plane_steps = plan(0, 0, field)
    return sorted({step[0] for step in weight_steps[group] + plane_steps})


def take(plan, me_ref, field, group, conv, mix, pieces, folded, target):
    section, place = me_ref[0], me_ref[1]
    taps = conv.shape[2] // 64
    fold_taps(conv.at[group, 0], 0, 0, taps, section, folded)
    fold_taps(mix.at[group, 0], 0, taps, 1, section, folded)
    weight_steps, plane_steps = plan(section, place, field)
    pieces = dict(zip(needed(plan, group, field), pieces, strict=True))
    for piece, start, count, layer, first, choices in weight_steps[group]:
        for choice in choices:

            @pl.when(first == choice)
            def _(piece=piece, start=start, count=count, layer=layer, choice=choice):
                fold_taps(pieces[piece], start, choice, count, layer, folded)

    for piece, start, rows, rel in plane_steps:
        row = pl.multiple_of((place ^ rel) * rows, rows)
        target[pl.ds(row, rows)] = pieces[piece][start : start + rows].astype(F32)


def begin(copies, sems, first):
    started = []
    for number, (source, target) in enumerate(copies):
        copy = pltpu.make_async_copy(source, target, sems.at[first + number])
        copy.start()
        started.append(copy)
    return started


def finish(started):
    for copy in started:
        copy.wait()


def split_kernel(me_ref, inputs, cotangent, token, own, beside, across, swap):
    chip, core = me_ref[1] // 2, me_ref[1] % 2
    old = lax.broadcasted_iota(jnp.int32, (128, 128), 0)
    new = lax.broadcasted_iota(jnp.int32, (128, 128), 1)
    order = ((old % 2) * 64 + old // 2 == new).astype(F32).astype(BF)
    for number, source in enumerate((inputs, cotangent)):
        rows = slice(128 * number, 128 * number + 128)

        def turned(offset, source=source):
            return dot(source[chip ^ offset], order, TN).astype(BF)

        mine, far = turned(0), turned(3)
        one, two = turned(1 + core), turned(2 - core)
        own[rows] = mine
        across[rows] = far
        beside[rows] = one
        swap[rows] = mine
        swap[256 + 128 * number : 384 + 128 * number] = two


def first_kernel(plan, piece_count, me_ref, conv, mix, *refs):
    pieces, refs = refs[:piece_count], refs[piece_count:]
    act, folded, slope, keep_a, keep_h, mark = refs
    section = me_ref[0]
    take(plan, me_ref, 0, 0, conv, mix, pieces, folded, act)
    for slot in range(2):
        clear_edges(keep_a.at[slot])
    mark[...] = jnp.zeros_like(mark)

    def step(layer, carry):
        forward_layer(layer, jnp.where(layer == section, 0, 1), act, folded, slope, keep_a, keep_h)
        return carry

    lax.fori_loop(0, folded.shape[0] - 1, step, 0)


def next_kernel(me_ref, mark, folded, *refs):
    act, slope, keep_a, keep_h = refs[-4:]
    layer = folded.shape[0] - 1
    forward_layer(layer, jnp.where(layer == me_ref[0], 0, 1), act, folded, slope, keep_a, keep_h)


def all_back(shares, me_ref, last, up, grad, wide, folded, slope, keep_a, keep_h, terms, out):
    section, replica = me_ref[0], me_ref[2]
    sections = folded.shape[0]
    target = out if len(shares) > 1 else terms

    def back(i, carry):
        layer = sections - 1 - i
        spread_if = None if last else layer > 0
        backward_layer(
            shares, replica, layer, layer == section, up, grad, wide, folded, slope, keep_a, keep_h, target, spread_if
        )
        return carry

    lax.fori_loop(0, sections, back, 0)
    if len(shares) == 1:
        rows = out.shape[0]
        out[...] = terms[pl.ds(pl.multiple_of(replica * rows, rows), rows)]


def second_kernel(shares, plan, piece_count, me_ref, conv, mix, *refs):
    pieces, refs = refs[:piece_count], refs[piece_count:]
    act_in, up, out, folded, slope, keep_a, keep_h, act, wide, terms, grad = refs
    section = me_ref[0]
    act[...] = act_in[...]
    take(plan, me_ref, 1, 1, conv, mix, pieces, folded, up)
    for slot in range(2):
        clear_edges(keep_a.at[slot])
    clear_edges(wide)

    def step(layer, carry):
        forward_layer(layer, jnp.where(layer == section, 0, 1), act, folded, slope, keep_a, keep_h, layer < folded.shape[0] - 1)
        return carry

    lax.fori_loop(0, folded.shape[0], step, 0)
    all_back(shares, me_ref, True, up, grad, wide, folded, slope, keep_a, keep_h, terms, out)


def third_kernel(shares, me_ref, up_in, folded, slope, keep_a, keep_h, out, up, wide, terms, grad):
    up[...] = up_in[...]
    clear_edges(wide)
    all_back(shares, me_ref, False, up, grad, wide, folded, slope, keep_a, keep_h, terms, out)


def place_taps(taps, factor, value, whole):
    for number, tap in enumerate(taps):
        whole[64 * tap : 64 * tap + 64] = value[64 * number : 64 * number + 64] * factor


def send_whole(whole, conv, mix, group, sems):
    taps = conv.shape[2]
    copies = [(whole.at[pl.ds(row, taps // 3)], conv.at[group, 0, pl.ds(row, taps // 3)]) for row in range(0, taps, taps // 3)]
    finish(begin(copies + [(whole.at[pl.ds(taps, whole.shape[0] - taps)], mix.at[group, 0])], sems, 0))


def both_kernel(group, factor, me_ref, own_a, own_b, far_a, far_b, *refs):
    conv, mix, whole, sems = refs[-4:]
    first = me_ref[2] == 0
    own = own_a[...].astype(F32) + own_b[...].astype(F32)
    far = far_a[...].astype(F32) + far_b[...].astype(F32)
    place_taps(SHARES[0], factor, jnp.where(first, own, far), whole)
    place_taps(SHARES[1], factor, jnp.where(first, far, own), whole)
    send_whole(whole, conv, mix, group, sems)


def plain_kernel(group, factor, me_ref, terms, *refs):
    conv, mix, whole, sems = refs[-4:]
    place_taps(range(28), factor, terms[...].astype(F32), whole)
    send_whole(whole, conv, mix, group, sems)


def size_of(x):
    return math.prod(x.shape) * x.dtype.itemsize


def call(kernel, outs, scratch, traffic, *args, into=()):
    vmem = pl.BlockSpec(memory_space=pltpu.VMEM)
    far = pl.BlockSpec(memory_space=pl.ANY)
    specs = [pl.BlockSpec(memory_space=pltpu.SMEM)] + [vmem] * (len(args) - 1) + [vmem if kernel.func is next_kernel else far] * len(into)
    held = sum(size_of(x) for x in scratch if x.memory_space == pltpu.VMEM)
    passed = sum(size_of(x) for x in args) + sum(size_of(x) for x in outs)
    limit = held + held // 4 + 10 * MIB
    if held + passed > 30 * MIB:
        limit = 63 * MIB
    return pl.pallas_call(
        kernel,
        out_shape=outs,
        in_specs=specs,
        out_specs=[far if kernel.func in (both_kernel, plain_kernel) else vmem] * len(outs),
        scratch_shapes=scratch,
        input_output_aliases={len(args) + i: i for i in range(len(into))},
        compiler_params=pltpu.CompilerParams(vmem_limit_bytes=limit),
        cost_estimate=pl.CostEstimate(flops=traffic * 100, bytes_accessed=traffic, transcendentals=0),
    )(*args, *into)


def exchange(block, mask):
    count = lax.axis_size("space")
    return lax.ppermute(block, "space", [(i, i ^ mask) for i in range(count)])


def cross(block, first, second):
    count = lax.axis_size("space")
    return lax.ppermute(block, "space", [(i, i ^ (second if i % 2 else first)) for i in range(count)])


def after(x, *others):
    return lax.optimization_barrier((x, *others))[0]


def gather_paired(weights, fields, me, place):
    sections, space = lax.axis_size("section"), lax.axis_size("space")
    rows = weights.shape[1]
    half, quarter = rows // 2, rows // 4
    chip, core = place // 2, place % 2
    side = (chip // 2) ^ (chip % 2)
    mine = jnp.where(side == 0, weights[:, :half], weights[:, half:])
    part = lax.dynamic_slice_in_dim(mine, core * quarter, quarter, axis=1)
    route = []
    for s in range(sections):
        for j in range(space):
            target = (s + (-1 if j % 2 else 1)) % sections
            route.append((s * space + j, target * space + j))
    across = [(s, (s + 2) % sections) for s in range(sections)]
    token = exchange(mine[0, :16], 1)
    own, beside, diagonal, swap = call(
        functools.partial(split_kernel),
        [jax.ShapeDtypeStruct((count, 128), BF) for count in (256, 256, 256, 512)],
        [], MIB, me, *fields, token,
    )
    other = exchange(swap, 1)
    diagonal = exchange(diagonal, 6)
    near, far = [], []
    for group in range(2):
        near.append(lax.ppermute(after(mine[group], *near), ("section", "space"), route))
        far.append(lax.ppermute(after(part[group], *near[:group]), "section", across))
    sent = [beside, other[256:]]
    diagonal_far = exchange(diagonal, 1)
    here = [jnp.concatenate([near[g], far[g]] + (sent if g == 0 else []), axis=0) for g in range(2)]
    here[0] = after(here[0], diagonal)
    there = [cross(x, 2, 4) for x in here]
    late = exchange(here[1], 1)
    ready = after(there[0], late)
    pieces = [here[0], there[0], exchange(here[0], 1), exchange(ready[:half], 1), here[1], there[1], late, None]
    planes = [own, other, diagonal, diagonal_far, exchange(ready[half:], 1)]
    plane_rows = 128

    def plan(section, place, field):
        chip, core = place // 2, place % 2
        side = (chip // 2) ^ (chip % 2)

        def where(piece, row):
            return (12, row - half) if piece == 3 and row >= half else (piece, row)

        weight_steps = []
        for group in range(2):
            steps = []
            for swapped in range(2):
                source = core ^ swapped
                beside = lax.rem(section + sections - 1 + 2 * source, sections)
                across = lax.rem(section + 2, sections)
                for other in range(2):
                    piece = 4 * group + 2 * swapped + other
                    first = (side ^ other) * 14
                    steps.append((piece, 0, 14, beside, first, (0, 14)))
                    steps.append((*where(piece, half), 7, across, first + source * 7, (0, 7, 14, 21)))
            weight_steps.append(steps)
        plane_steps = []
        start = field * plane_rows
        for piece, rel in ((8, 0), (9, 1), (10, 6), (11, 7)):
            plane_steps.append((piece, start, plane_rows, rel))
        for swapped in range(2):
            rel = swapped ^ (2 + 2 * (core ^ swapped))
            start = half + quarter + field * plane_rows
            plane_steps.append((*where(1 + 2 * swapped, start), plane_rows, rel))
            plane_steps.append((*where(1 + 2 * swapped, start + 2 * plane_rows), plane_rows, rel ^ 1))
        return weight_steps, plane_steps

    return pieces + planes, plan


def gather_plain(weights, both, place, replicas):
    sections = lax.axis_size("section")
    micro_count, _, plane_rows, _ = both.shape
    routes = [[(i, (i + d) % sections) for i in range(sections)] for d in range(1, sections)]
    pieces = [lax.ppermute(group, "section", route) for group in weights for route in routes]
    near = []
    for k in range(micro_count):
        part = lax.dynamic_index_in_dim(both, (place // replicas) ^ k, 0, keepdims=False)
        near.append(part if k == 0 else exchange(part, k * replicas))
    near = jnp.stack(near)
    fields = [near] + [exchange(near, r) for r in range(1, replicas)]
    fields = [x.reshape(-1, x.shape[-1]) for x in fields]

    def plan(section, place, field):
        first = weights.shape[0] * (sections - 1)
        weight_steps = [
            [
                (group * (sections - 1) + d - 1, 0, weights.shape[1] // 64, lax.rem(section + sections - d, sections), 0, (0,))
                for d in range(1, sections)
            ]
            for group in range(weights.shape[0])
        ]
        plane_steps = [
            (first + r, (2 * k + field) * plane_rows, plane_rows, k * replicas + r)
            for k in range(micro_count)
            for r in range(replicas)
        ]
        return weight_steps, plane_steps

    return pieces + fields, plan


def per_device(inputs, cotangent, conv_weight, mix_weight):
    micro_count, channels, extent_x, extent_y, extent_z = inputs.shape
    groups, _, hidden, taps = conv_weight.shape
    sections = lax.axis_size("section")
    space = lax.axis_size("space")
    section = lax.axis_index("section")
    place = lax.axis_index("space")
    replicas = space // micro_count
    width = taps + channels
    layers = groups * sections
    cells = extent_x * space * extent_z
    lanes = extent_y * channels
    paired = space == 8 and replicas == 2 and sections == 4 and extent_x == 1 and extent_z == 128 and lanes == 128
    me = jnp.stack([section, place, place % replicas]).astype(jnp.int32)

    conv_rows = jnp.swapaxes(conv_weight, 2, 3)
    weights = jnp.concatenate([conv_rows[:, 0], mix_weight[:, 0]], axis=1)
    if paired:
        fields = [x.reshape(micro_count, lanes, extent_z) for x in (inputs, cotangent)]
        pieces, plan = gather_paired(weights, fields, me, place)
    else:
        both = jnp.stack([inputs, cotangent], axis=1)
        both = both.transpose(0, 1, 3, 5, 4, 2).reshape(micro_count, 2, extent_x * extent_z, lanes)
        pieces, plan = gather_plain(weights, both, place, replicas)

    total_x = extent_x * space
    act = jax.ShapeDtypeStruct((cells, lanes), F32)
    kept = [
        jax.ShapeDtypeStruct((sections, 10 * lanes, 2 * hidden), BF),
        jax.ShapeDtypeStruct((sections, cells, 2 * hidden), BF),
        jax.ShapeDtypeStruct((2, total_x + 2, extent_z, 3 * lanes), BF),
        jax.ShapeDtypeStruct((2, cells, 2 * hidden), BF),
    ]
    early = [pieces[i] for i in needed(plan, 0, 0)]
    act, folded, *state, mark = call(
        functools.partial(first_kernel, plan, len(early)),
        [act] + kept + [jax.ShapeDtypeStruct((8, 128), F32)],
        [], 2 * MIB,
        me, conv_rows, mix_weight, *early,
    )
    act, *state = call(
        functools.partial(next_kernel), [act] + kept[1:], [], 2 * MIB, me, mark, folded, into=(act, *state)
    )
    saved = (folded, *state)
    if paired:
        pieces[7] = exchange(after(pieces[5], mark), 1)
    late = [pieces[i] for i in needed(plan, 1, 1)]
    terms = jax.ShapeDtypeStruct((width // replicas, hidden), BF)
    shares = SHARES if paired else (tuple(range(28)),)
    wide = pltpu.VMEM((total_x + 2, extent_z, 9 * lanes), F32)
    whole = pltpu.VMEM((width, hidden), BF)
    grad = pltpu.VMEM((cells, 2 * hidden), BF)
    up, late_terms = call(
        functools.partial(second_kernel, shares, plan, len(late)),
        [act, terms],
        [pltpu.VMEM(x.shape, x.dtype) for x in kept] + [pltpu.VMEM((cells, lanes), F32), wide, whole, grad],
        40 * MIB,
        me, conv_rows, mix_weight, *late, act,
    )
    traded = cross(late_terms, 2, 4) if paired else None
    (early_terms,) = call(
        functools.partial(third_kernel, shares),
        [terms],
        [pltpu.VMEM((cells, lanes), F32), wide, whole, grad],
        20 * MIB,
        me, up, *saved,
    )

    factor = 1.0 / math.sqrt(micro_count * cells * extent_y)
    outs = [
        jax.ShapeDtypeStruct((groups, 1, taps, hidden), F32),
        jax.ShapeDtypeStruct((groups, 1, channels, hidden), F32),
    ]
    scratch = [pltpu.VMEM((width, hidden), F32), pltpu.SemaphoreType.DMA((4,))]
    grads = ()
    for group in (1, 0):
        own = late_terms if group else early_terms
        if paired:
            met = after(traded, early_terms) if group else cross(own, 2, 4)
            half = (own.astype(F32) + met.astype(F32)).astype(BF)
            other = cross(half, 4, 2)
            if grads:
                other = after(other, grads[0])
            kernel, parts = both_kernel, (half, other, exchange(half, 1), exchange(other, 1))
        else:
            level = [own] + [exchange(own, k * replicas) for k in range(1, micro_count)]
            level = [x.astype(F32) for x in level]
            while len(level) > 1:
                level = [level[i] + level[i + 1] for i in range(0, len(level), 2)]
            rows_of = [[m * replicas + r for r in range(replicas)] for m in range(micro_count)]
            every = lax.all_gather(level[0].astype(BF), "space", axis=0, tiled=True, axis_index_groups=rows_of)
            kernel, parts = plain_kernel, (every,)
        grads = call(functools.partial(kernel, group, factor), outs, scratch, MIB // 16, me, *parts, into=grads)
    conv, mix = grads
    return (jnp.swapaxes(conv, 2, 3), mix)


def solution(mesh):
    placed = (
        P(None, None, "space", None, None),
        P(None, None, "space", None, None),
        P(None, "section", None, None),
        P(None, "section", None, None),
    )
    return jax.shard_map(
        per_device,
        mesh=mesh,
        in_specs=placed,
        out_specs=(P(None, "section", None, None), P(None, "section", None, None)),
        check_vma=False,
    )
```
